512 devices in a mesh: dp: 32 (over x, y), seq: 16 (over z, core).
Axes of the slice: x: 4, y: 8, z: 8, core: 2. Of those that a mesh axis runs over, the one named last changes fastest.
Arguments:
- queries: bfloat16 [65536, 2048], P(('dp', 'seq')), may hold values from -6 to 6
- keys: bfloat16 [65536, 2048], P(('dp', 'seq')), may hold values from -6 to 6
- values: bfloat16 [65536, 2048], P(('dp', 'seq')), may hold values from -6 to 6
- text_kv: bfloat16 [256, 256, 2, 2048], P('dp', None, None, 'seq'), may hold values from -6 to 6
- text_lengths: int32 [256], P('dp'), may hold values from 1 to 256
- clip_lengths: int32 [32, 8], P('dp'), may hold values from 1 to 512, 2048 in all within a row
- timesteps: int32 [256], P('dp'), may hold values from 0 to 999
- mod_weight: bfloat16 [256, 4096], replicated, may hold values from -0.375 to 0.375
- final_weight: bfloat16 [2048, 64], replicated, may hold values from -0.125 to 0.125
- noise: float32 [65536, 64], P(('dp', 'seq')), may hold values from -6 to 6
- clean: float32 [65536, 64], P(('dp', 'seq')), may hold values from -12 to 12
- report_order: int32 [256], P('dp'), may hold values from 0 to 255, each once
Outputs:
- scores: float32 [256], P('dp')
The draws below stay inside these ranges and needn't reach their ends.
Inputs may be any that keep to these rules, and one draw needn't show every extreme that they name: Each row of clip_lengths sums to 2048, and its largest entry is exactly 512.
All inputs are finite; a program needn't handle non-finite values.
Results may differ from the reference program's by a relative error of at most 0.00055.
Values may be sent and summed in bfloat16 or wider, within the bound.
A program may use at most 64 MiB of HBM per device.

```python
import math
import jax
import jax.numpy as jnp
import numpy as np
from jax import lax

HEADS = 16
HEAD_DIM = 128
CHANNELS = 64
TEXT_LEN = 256
FREQ = 256
STEPS = 1000
TOK_DEV = 128
CLIPS_GRP = 8
WIDTH = 2048
GROUPS = 32
GRP_TOK = 2048
CLIP_MOST = 512
TOKENS = 65536
CLIPS = 256
N_DP = 32
N_SEQ = 16


def drawn_rows(key):
    return jnp.clip(jax.random.normal(key, (TOKENS, HEADS * HEAD_DIM), jnp.float32), -6.0, 6.0)


def draw_queries(key, part):
    key = jax.random.fold_in(key, 11)
    drawn = drawn_rows(key)
    return drawn.astype(jnp.bfloat16)


def draw_keys(key, part):
    key = jax.random.fold_in(key, 23)
    drawn = drawn_rows(key)
    return drawn.astype(jnp.bfloat16)


def draw_clean(key, part):
    key = jax.random.fold_in(key, 37)
    key_base, key_rows, key_cols = jax.random.split(key, 3)
    row_scale = jnp.exp(jax.random.uniform(key_rows, (TOKENS, 1), jnp.float32, -1.15, 1.15))
    col_scale = jnp.exp(jax.random.uniform(key_cols, (1, CHANNELS), jnp.float32, -0.6, 0.6))
    base = jax.random.normal(key_base, (TOKENS, CHANNELS), jnp.float32)
    return jnp.clip(base * row_scale * col_scale, -12.0, 12.0)


def plant(array, stream_key, low, largest):
    longest = array.shape.index(max(array.shape))
    spots = []
    for shift in (0, 1):
        where = [jax.random.randint(jax.random.fold_in(stream_key, axis), (), 0, length) for axis, length in enumerate(array.shape)]
        where[longest] = (where[longest] + shift) % array.shape[longest]
        spots.append(tuple(where))
    return array.at[spots[0]].set(low).at[spots[1]].set(largest)


def levels(stream_key, shape, shards, least, top_value):
    loudness = 1.0
    for dim, shards_of in shards:
        draws = jax.random.uniform(jax.random.fold_in(jax.random.fold_in(stream_key, 6), dim), (shards_of,), jnp.float32, least / len(shards), top_value / len(shards))
        loudness = loudness * jnp.repeat(jnp.exp(draws), shape[dim] // shards_of).reshape((-1,) + (1,) * (len(shape) - 1 - dim))
    return loudness


def split_up(number_of, total, reach, lean):
    portions = [(1 << 20) // math.isqrt(standing ** lean) + 1 for standing in range(2, number_of + 1)]
    rest, holding = total - reach - (number_of - 1), [1] * (number_of - 1)
    while rest > 0:
        movable = [i for i in range(number_of - 1) if holding[i] < reach]
        whole, remaining = sum([portions[i] for i in movable]), rest
        for i in movable:
            more = min(reach - holding[i], max(1, remaining * portions[i] // whole), rest)
            holding[i] = holding[i] + more
            rest = rest - more
    return np.array([reach] + holding)


def uneven_parts(rng, amount, total, limit, skew):
    if amount == 2:
        one = jax.random.randint(rng, (), max(1, total - limit), min(limit, total - 1) + 1)
        return jnp.stack([one, total - one])
    sizes = jnp.asarray(split_up(amount, total, limit, skew), jnp.int32)
    twos = (amount - 1) // 2
    donor, receiver = sizes[1:1 + 2 * twos:2], sizes[2:2 + 2 * twos:2]
    slack = jnp.minimum(donor - 1, limit - receiver)
    passed = jax.random.randint(jax.random.fold_in(rng, 1), (twos,), 0, 1 << 20) % (slack + 1)
    sizes = sizes.at[1:1 + 2 * twos:2].set(donor - passed).at[2:2 + 2 * twos:2].set(receiver + passed)
    return sizes[jax.random.permutation(jax.random.fold_in(rng, 2), amount)]


def scatter_about(own_key, dims, deviation, most, cuts=(), kind=jnp.bfloat16):
    loudness = levels(own_key, dims, cuts, -0.22, 0.18) if cuts else 1.0
    entries = jax.random.normal(own_key, dims, jnp.float32) * deviation * loudness
    return jnp.minimum(jnp.maximum(entries, -most), most).astype(kind)


def setup_inputs(seed: int = 0) -> dict:
    splits = jax.random.split(jax.random.key(seed), 13)
    queries = draw_queries(jax.random.fold_in(splits[12], 71), 0)
    keys = draw_keys(jax.random.fold_in(splits[12], 71), 0)
    values = scatter_about(splits[2], (TOKENS, WIDTH), 1.0, 6.0, ((0, 512),))
    text_kv = scatter_about(splits[3], (CLIPS, TEXT_LEN, 2, WIDTH), 1.0, 6.0, ((0, 32), (3, 16)))
    text_lengths = plant(jax.random.randint(splits[4], (CLIPS,), 1, TEXT_LEN + 1), jax.random.fold_in(splits[4], 1), 1, TEXT_LEN).astype(jnp.int32)
    clip_lengths = jax.vmap(lambda own: uneven_parts(own, CLIPS_GRP, GRP_TOK, CLIP_MOST, 2))(jax.random.split(splits[5], GROUPS)).reshape((GROUPS, CLIPS_GRP)).astype(jnp.int32)
    timesteps = plant(jax.random.randint(splits[6], (CLIPS,), 0, STEPS), jax.random.fold_in(splits[6], 1), 0, STEPS - 1).astype(jnp.int32)
    mod_weight = scatter_about(splits[7], (FREQ, 2 * WIDTH), FREQ ** -0.5, 0.375)
    final_weight = scatter_about(splits[8], (WIDTH, CHANNELS), WIDTH ** -0.5, 0.125)
    noise = scatter_about(splits[9], (TOKENS, CHANNELS), 1.0, 6.0, ((0, 512),), jnp.float32)
    clean = draw_clean(jax.random.fold_in(splits[12], 71), 0)
    report_order = jax.random.permutation(splits[11], CLIPS).astype(jnp.int32)
    return dict(queries=queries, keys=keys, values=values, text_kv=text_kv, text_lengths=text_lengths, clip_lengths=clip_lengths, timesteps=timesteps, mod_weight=mod_weight, final_weight=final_weight, noise=noise, clean=clean, report_order=report_order)


def step_embedding(timesteps):
    half_width = FREQ // 2
    frequency = jnp.exp(-math.log(10000.0) * jnp.arange(half_width, dtype=jnp.float32) / half_width)
    angles = timesteps.astype(jnp.float32)[:, None] * frequency[None, :]
    return jnp.concatenate([jnp.cos(angles), jnp.sin(angles)], axis=1)

def reference(queries, keys, values, text_kv, text_lengths, clip_lengths, timesteps, mod_weight, final_weight, noise, clean, report_order):
    group_rows = TOK_DEV * N_SEQ
    feat_width = HEADS * HEAD_DIM
    inverse_root = 1.0 / math.sqrt(HEAD_DIM)
    activated = jax.nn.silu(step_embedding(timesteps)).astype(jnp.bfloat16)
    modulation = jnp.dot(activated, mod_weight, preferred_element_type=jnp.float32)
    weight_full = final_weight.astype(jnp.float32)

    def one_group(group_rank):
        group_rank = group_rank.astype(jnp.int32)
        lengths = clip_lengths[group_rank]
        clip_ends = jnp.cumsum(lengths).astype(jnp.int32)
        places = jnp.arange(group_rows, dtype=jnp.int32)
        clip_of = lax.optimization_barrier(jnp.sum((places[:, None] >= clip_ends[None, :]).astype(jnp.int32), axis=1))
        first_row = (group_rank * group_rows).astype(jnp.int32)
        first_clip = (group_rank * CLIPS_GRP).astype(jnp.int32)
        query_rows = lax.dynamic_slice_in_dim(queries, first_row, group_rows, 0)
        key_rows = lax.dynamic_slice_in_dim(keys, first_row, group_rows, 0)
        value_rows = lax.dynamic_slice_in_dim(values, first_row, group_rows, 0)
        text_rows = lax.dynamic_slice_in_dim(text_kv, first_clip, CLIPS_GRP, 0)
        text_count = lax.dynamic_slice_in_dim(text_lengths, first_clip, CLIPS_GRP, 0)
        text_slots = jnp.arange(CLIPS_GRP * TEXT_LEN, dtype=jnp.int32)
        text_clip = text_slots // TEXT_LEN
        text_live = text_slots % TEXT_LEN < text_count[text_clip]
        live_mask = jnp.concatenate([clip_of[:, None] == clip_of[None, :], (clip_of[:, None] == text_clip[None, :]) & text_live[None, :]], axis=1)
        keys_all = jnp.concatenate([key_rows, text_rows[:, :, 0, :].reshape(CLIPS_GRP * TEXT_LEN, feat_width)], axis=0)
        values_all = jnp.concatenate([value_rows, text_rows[:, :, 1, :].reshape(CLIPS_GRP * TEXT_LEN, feat_width)], axis=0)
        query_split = query_rows.reshape(group_rows, HEADS, HEAD_DIM).transpose(1, 0, 2)
        key_split = keys_all.reshape(-1, HEADS, HEAD_DIM).transpose(1, 0, 2)
        value_split = values_all.reshape(-1, HEADS, HEAD_DIM).transpose(1, 0, 2)

        def one_head(items):
            query_head, key_head, value_head = items
            score_rows = jnp.dot(query_head, key_head.T, preferred_element_type=jnp.float32) * inverse_root
            score_rows = jnp.where(live_mask, score_rows, -jnp.inf)
            row_top = lax.optimization_barrier(jnp.max(score_rows, axis=1, keepdims=True))
            weights = jnp.exp(score_rows - row_top)
            weights = (weights / lax.optimization_barrier(jnp.sum(weights, axis=1, keepdims=True))).astype(jnp.bfloat16)
            return jnp.dot(weights, value_head, preferred_element_type=jnp.float32).astype(jnp.bfloat16)
        head_out = lax.map(one_head, (query_split, key_split, value_split))
        attended = head_out.transpose(1, 0, 2).reshape(group_rows, feat_width)
        values_full = attended.astype(jnp.float32)
        center = lax.optimization_barrier(jnp.mean(values_full, axis=1, keepdims=True))
        spread = lax.optimization_barrier(jnp.mean(values_full * values_full, axis=1, keepdims=True)) - center * center
        normed = (values_full - center) * lax.rsqrt(spread + 1e-06)
        group_mods = lax.dynamic_slice_in_dim(modulation, first_clip, CLIPS_GRP, 0)[clip_of]
        modulated = normed * (1.0 + group_mods[:, feat_width:]) + group_mods[:, :feat_width]
        predicted = jnp.dot(modulated, weight_full, precision=lax.Precision.HIGHEST)
        target = lax.dynamic_slice_in_dim(noise, first_row, group_rows, 0) - lax.dynamic_slice_in_dim(clean, first_row, group_rows, 0)
        difference = predicted - target
        error_rows = lax.optimization_barrier(jnp.mean(difference * difference, axis=1))
        token_picks = clip_of[:, None] == jnp.arange(CLIPS_GRP, dtype=jnp.int32)[None, :]
        clip_totals = lax.optimization_barrier(jnp.sum(jnp.where(token_picks, error_rows[:, None], 0.0), axis=0))
        return clip_totals / lengths.astype(jnp.float32)
    clip_loss = lax.map(one_group, jnp.arange(N_DP, dtype=jnp.int32)).reshape(-1)
    return clip_loss[report_order]
```

```python
import functools
import math

import jax
import jax.numpy as jnp
from jax import lax
from jax.experimental import pallas as pl
from jax.experimental.pallas import tpu as pltpu
from jax.sharding import PartitionSpec as P

MESH = pl.DeviceIdType.MESH
HEAD_DIM = 128
FREQ = 256
CLIPS = 8
TEXT = 256
CHANNELS = 64
WIDTH = 2048
TOK = 128
N_SEQ = 16
N_DP = 32
ROWS = TOK * N_SEQ
BLOCK = 256
BLOCKS = ROWS // BLOCK
PAD = 512
WINDOW = BLOCK + 2 * PAD
NEAR_CLIPS = 5
SPAN = NEAR_CLIPS * TEXT
MSG = 80
FAR = 65536.0
EPS = 1e-06
SCALE = math.log2(math.e) / math.sqrt(HEAD_DIM)
NT = (((1,), (1,)), ((), ()))
F32 = jnp.float32
BF16 = jnp.bfloat16


def step_embedding(timesteps):
    half_width = FREQ // 2
    frequency = jnp.exp(-math.log(10000.0) * jnp.arange(half_width, dtype=F32) / half_width)
    angles = timesteps.astype(F32)[:, None] * frequency[None, :]
    return jnp.concatenate([jnp.cos(angles), jnp.sin(angles)], axis=1)


def nt_dot(a, b):
    return lax.dot_general(a, b, NT, preferred_element_type=F32)


def nn_dot(a, b):
    return jnp.dot(a, b, preferred_element_type=F32)


def pieces(x, count):
    out = []
    for _ in range(count):
        piece = x.astype(BF16)
        out.append(piece)
        x = x - piece.astype(F32)
    return out


def along(scalars, shape, dim):
    place = lax.broadcasted_iota(jnp.int32, shape, dim)
    out = jnp.zeros(shape, jnp.int32)
    for index, scalar in enumerate(scalars):
        out = jnp.where(place == index, scalar, out)
    return out


PARTNERS = [(4, 1), (4, 0), (3, 0), (-3, 0), (3, 1), (-3, 1), (2, 0), (-2, 0), (2, 1), (-2, 1)]
PARTNERS += [(1, 0), (-1, 0), (1, 1), (-1, 1), (0, 1)]


def kernel(
    q_hbm, k_hbm, v_hbm, text_hbm, act_ref, tlen_ref, clen_ref, order_ref, modw_hbm, finw_hbm, noise_hbm, clean_hbm,
    out_ref,
    qbuf, kbuf, vbuf, textbuf, modw, finw, noise, clean,
    tk, tv, qbias, kbias, tbias, onehot, clip_row, wall, btok, ctok, target,
    text_max, text_sum, text_out, inverse, weights, message, gathered, part_out, part_in, loss_out, loss_in,
    in_send, in_recv, own_sem, load_sem, msg_send, msg_recv, part_send, part_recv, loss_send, loss_recv,
):
    me = lax.axis_index("seq")
    dp = lax.axis_index("dp")
    z = me // 2
    core = me % 2
    peers = [lax.rem(z + dz + 8, 8) * 2 + lax.rem(core + dc, 2) for dz, dc in PARTNERS]

    loads = [
        pltpu.make_async_copy(src, dst, load_sem.at[i])
        for i, (src, dst) in enumerate(
            [(text_hbm, textbuf), (modw_hbm, modw), (finw_hbm, finw), (noise_hbm, noise), (clean_hbm, clean)]
        )
    ]
    for load in loads:
        load.start()
    own = []
    for t, (src, dst, base) in enumerate([(q_hbm, qbuf, 0), (k_hbm, kbuf, PAD), (v_hbm, vbuf, PAD)]):
        own.append(
            pltpu.make_async_copy(
                src.at[:, pl.ds(pl.multiple_of(me * HEAD_DIM, HEAD_DIM), HEAD_DIM)],
                dst.at[pl.ds(pl.multiple_of(base + me * TOK, TOK), TOK)],
                own_sem.at[t],
            )
        )
        own[-1].start()

    barrier = pltpu.get_barrier_semaphore()
    for peer in peers:
        pl.semaphore_signal(barrier, inc=1, device_id=(dp, peer), device_id_type=MESH)
    for i in range(1, N_DP):
        pl.semaphore_signal(barrier, inc=1, device_id=(lax.rem(dp + i, N_DP), me), device_id_type=MESH)
    pl.semaphore_wait(barrier, N_SEQ - 1 + N_DP - 1)

    sends = []
    for t, (src, dst, base) in enumerate([(q_hbm, qbuf, 0), (k_hbm, kbuf, PAD), (v_hbm, vbuf, PAD)]):
        row = []
        for j, peer in enumerate(peers):
            copy = pltpu.make_async_remote_copy(
                src_ref=src.at[:, pl.ds(pl.multiple_of(peer * HEAD_DIM, HEAD_DIM), HEAD_DIM)],
                dst_ref=dst.at[pl.ds(pl.multiple_of(base + me * TOK, TOK), TOK)],
                send_sem=in_send.at[t, j],
                recv_sem=in_recv.at[t, j],
                device_id=(dp, peer),
                device_id_type=MESH,
            )
            copy.start()
            row.append(copy)
        sends.append(row)

    starts, ends = [], []
    total = jnp.int32(0)
    for c in range(CLIPS):
        starts.append(total)
        total = total + clen_ref[0, c]
        ends.append(total)
    start_lane, end_lane = along(starts, (1, HEAD_DIM), 1), along(ends, (1, HEAD_DIM), 1)
    start_col, end_col = along(starts, (CLIPS, 1), 0), along(ends, (CLIPS, 1), 0)
    size_col = (end_col - start_col).astype(F32)
    place = lax.broadcasted_iota(jnp.int32, (CLIPS, ROWS), 1)
    onehot[...] = jnp.where((place >= start_col) & (place < end_col), 1.0, 0.0)
    clip_of = jnp.zeros((CLIPS, ROWS), jnp.int32)
    for c in range(1, CLIPS):
        clip_of = clip_of + jnp.where(place >= starts[c], 1, 0)
    clip_row[...] = clip_of
    edge = jnp.zeros((PAD, HEAD_DIM), BF16)
    for buf in (kbuf, vbuf):
        buf[pl.ds(0, PAD), :] = edge
        buf[pl.ds(PAD + ROWS, PAD), :] = edge

    rows_iota = lax.broadcasted_iota(jnp.int32, (BLOCK, HEAD_DIM), 0)
    lane_iota = lax.broadcasted_iota(jnp.int32, (BLOCK, HEAD_DIM), 1)

    def fill_key_bias(i, _):
        token = rows_iota + (i * BLOCK - PAD)
        live = (token >= start_lane) & (token < end_lane)
        kbias[pl.ds(pl.multiple_of(i * BLOCK, BLOCK), BLOCK), :] = jnp.where(live, 0.0, -FAR).astype(BF16)
        return 0

    def fill_query_bias(i, _):
        token = rows_iota + i * BLOCK
        live = (token >= start_lane) & (token < end_lane)
        qbias[pl.ds(pl.multiple_of(i * BLOCK, BLOCK), BLOCK), :] = jnp.where(live, 1.0, 0.0).astype(BF16)
        return 0

    lax.fori_loop(0, (ROWS + 2 * PAD) // BLOCK, fill_key_bias, 0)
    lax.fori_loop(0, BLOCKS, fill_query_bias, 0)

    loads[0].wait()
    sub = lax.broadcasted_iota(jnp.int32, (TEXT, 2 * TEXT), 0)
    lane = lax.broadcasted_iota(jnp.int32, (TEXT, 2 * TEXT), 1)
    pick_key = jnp.where(lane == 2 * sub, 1.0, 0.0).astype(BF16)
    pick_value = jnp.where(lane == 2 * sub + 1, 1.0, 0.0).astype(BF16)
    length_lane = along([tlen_ref[c] for c in range(CLIPS)], (1, HEAD_DIM), 1)

    def split_text(c, _):
        both = textbuf[c]
        rows = pl.ds(pl.multiple_of(c * TEXT, TEXT), TEXT)
        tk[rows, :] = nn_dot(pick_key, both).astype(BF16)
        tv[rows, :] = nn_dot(pick_value, both).astype(BF16)
        live = (lane_iota == c) & (rows_iota < length_lane)
        tbias[rows, :] = jnp.where(live, 0.0, -FAR).astype(BF16)
        return 0

    lax.fori_loop(0, CLIPS, split_text, 0)

    loads[1].wait()
    loads[2].wait()
    act = act_ref[...]
    head_at = pl.multiple_of(me * HEAD_DIM, HEAD_DIM)
    gain = 1.0 + nn_dot(act, modw[:, pl.ds(WIDTH + head_at, HEAD_DIM)])
    turned = finw[:, pl.ds(head_at, HEAD_DIM)].astype(F32)
    for c in range(CLIPS):
        high, low = pieces(turned * gain[c : c + 1, :], 2)
        wall[pl.ds(c * CHANNELS, CHANNELS), :] = jnp.concatenate([high, low], axis=1)
    shift_all = nn_dot(act, modw[:, pl.ds(0, WIDTH)])
    gain_all = 1.0 + nn_dot(act, modw[:, pl.ds(WIDTH, WIDTH)])
    stacked = jnp.concatenate(pieces(gain_all, 3) + pieces(shift_all, 3), axis=0)
    folded = nt_dot(finw[...], stacked)
    gain_sum = folded[:, 0:8] + folded[:, 8:16] + folded[:, 16:24]
    shift_sum = folded[:, 24:32] + folded[:, 32:40] + folded[:, 40:48]
    mine = onehot[:, pl.ds(pl.multiple_of(me * TOK, TOK), TOK)]
    gain_tok = jnp.zeros((CHANNELS, TOK), F32)
    shift_tok = jnp.zeros((CHANNELS, TOK), F32)
    for c in range(CLIPS):
        gain_tok = gain_tok + gain_sum[:, c : c + 1] * mine[c : c + 1, :]
        shift_tok = shift_tok + shift_sum[:, c : c + 1] * mine[c : c + 1, :]
    btok[...] = gain_tok
    ctok[...] = shift_tok
    loads[3].wait()
    loads[4].wait()
    target[...] = noise[...] - clean[...]
    order_lane = along([order_ref[c] for c in range(CLIPS)], (1, HEAD_DIM), 1)

    own[0].wait()
    for copy in sends[0]:
        copy.wait_recv()
    one_lanes = jnp.ones((SPAN, HEAD_DIM), BF16)

    def text_block(b, _):
        rows = pl.ds(pl.multiple_of(b * BLOCK, BLOCK), BLOCK)
        span = pl.ds(pl.multiple_of(b // 2 * TEXT, TEXT), SPAN)
        left = jnp.concatenate([qbuf[rows, :], qbias[rows, :]], axis=1)
        right = jnp.concatenate([tk[span, :], tbias[span, :]], axis=1)
        scores = nt_dot(left, right)
        top = jnp.max(scores, axis=1, keepdims=True)
        weight = jnp.exp2((scores - top) * SCALE).astype(BF16)
        mixed = nn_dot(weight, jnp.concatenate([tv[span, :], one_lanes], axis=1))
        text_max[rows, :] = jnp.broadcast_to(top, (BLOCK, HEAD_DIM))
        text_out[rows, :] = mixed[:, :HEAD_DIM]
        text_sum[rows, :] = mixed[:, HEAD_DIM:]
        return 0

    lax.fori_loop(0, BLOCKS, text_block, 0)

    own[1].wait()
    for copy in sends[1]:
        copy.wait_recv()
    one_wide = jnp.ones((WINDOW, HEAD_DIM), BF16)

    def score_block(b, _):
        rows = pl.ds(pl.multiple_of(b * BLOCK, BLOCK), BLOCK)
        window = pl.ds(pl.multiple_of(b * BLOCK, BLOCK), WINDOW)
        left = jnp.concatenate([qbuf[rows, :], qbias[rows, :]], axis=1)
        right = jnp.concatenate([kbuf[window, :], kbias[window, :]], axis=1)
        scores = nt_dot(left, right)
        before = text_max[rows, :]
        top = jnp.maximum(before, jnp.max(scores, axis=1, keepdims=True))
        weight = jnp.exp2((scores - top[:, :1]) * SCALE).astype(BF16)
        weights[rows, :] = weight
        fade = jnp.exp2((before - top) * SCALE)
        inv = 1.0 / (nn_dot(weight, one_wide) + text_sum[rows, :] * fade)
        inverse[rows, :] = inv
        text_out[rows, :] = text_out[rows, :] * (fade * inv)
        return 0

    lax.fori_loop(0, BLOCKS, score_block, 0)

    own[2].wait()
    for copy in sends[2]:
        copy.wait_recv()
    ones_row = jnp.ones((8, 2 * HEAD_DIM), BF16)
    row8 = lax.broadcasted_iota(jnp.int32, (8, TOK), 0)

    def message_copy(owner):
        return pltpu.make_async_remote_copy(
            src_ref=message.at[owner],
            dst_ref=gathered.at[me],
            send_sem=msg_send.at[owner],
            recv_sem=msg_recv.at[me],
            device_id=(dp, owner),
            device_id_type=MESH,
        )

    def value_block(i, _):
        reach = (i + 1) // 2
        step = 4 + reach - 2 * reach * lax.rem(i, 2)
        b = lax.rem(z + step, 8)
        rows = pl.ds(pl.multiple_of(b * BLOCK, BLOCK), BLOCK)
        window = pl.ds(pl.multiple_of(b * BLOCK, BLOCK), WINDOW)
        first = b // 2
        mixed = nn_dot(weights[rows, :], vbuf[window, :])
        attended = (mixed * inverse[rows, :] + text_out[rows, :]).astype(BF16)
        fold = wall[pl.ds(pl.multiple_of(first * CHANNELS, CHANNELS), NEAR_CLIPS * CHANNELS), :]
        for half in range(2):
            owner = 2 * b + half
            part = attended[half * TOK : (half + 1) * TOK]
            spread = nt_dot(fold, jnp.concatenate([part, part], axis=1))
            picked = jnp.zeros((CHANNELS, TOK), F32)
            clip_here = clip_row[0:1, pl.ds(pl.multiple_of(owner * TOK, TOK), TOK)]
            for j in range(NEAR_CLIPS):
                picked = jnp.where(clip_here == first + j, spread[j * CHANNELS : (j + 1) * CHANNELS], picked)
            wide_part = part.astype(F32)
            total = nt_dot(ones_row[:, :HEAD_DIM], part)
            squares = nt_dot(ones_row, jnp.concatenate(pieces(wide_part * wide_part, 2), axis=1))
            total_high, total_low = [x.astype(F32) for x in pieces(total, 2)]
            square_high, square_low = [x.astype(F32) for x in pieces(squares, 2)]
            stats = jnp.where(row8 == 0, total_high, jnp.where(row8 == 1, total_low, jnp.where(row8 == 2, square_high, square_low)))
            message[owner] = jnp.concatenate([picked, stats, jnp.zeros((8, TOK), F32)], axis=0).astype(BF16)

            @pl.when(owner != me)
            def _():
                message_copy(owner).start()

        return 0

    lax.fori_loop(0, BLOCKS, value_block, 0)

    total = message[me].astype(F32)
    for peer in peers:
        pltpu.make_async_remote_copy(
            src_ref=message.at[peer],
            dst_ref=gathered.at[peer],
            send_sem=msg_send.at[peer],
            recv_sem=msg_recv.at[peer],
            device_id=(dp, peer),
            device_id_type=MESH,
        ).wait_recv()
        total = total + gathered[peer].astype(F32)
    center = (total[64:65] + total[65:66]) / WIDTH
    spread = (total[66:67] + total[67:68]) / WIDTH - center * center
    predicted = lax.rsqrt(spread + EPS) * (total[:CHANNELS] - center * btok[...]) + ctok[...]
    difference = predicted - target[...]
    error = jnp.sum(difference * difference, axis=0, keepdims=True) / CHANNELS
    mine = onehot[:, pl.ds(pl.multiple_of(me * TOK, TOK), TOK)]
    partial = jnp.broadcast_to(jnp.sum(mine * error, axis=1, keepdims=True), (CLIPS, HEAD_DIM))
    part_out[...] = partial
    parts = []
    for j, peer in enumerate(peers):
        copy = pltpu.make_async_remote_copy(
            src_ref=part_out,
            dst_ref=part_in.at[j],
            send_sem=part_send.at[j],
            recv_sem=part_recv.at[j],
            device_id=(dp, peer),
            device_id_type=MESH,
        )
        copy.start()
        parts.append(copy)
    for j, copy in enumerate(parts):
        copy.wait_recv()
        partial = partial + part_in[j]
    losses = partial / size_col
    loss_out[...] = losses
    lefts = []
    for i in range(1, N_DP):
        copy = pltpu.make_async_remote_copy(
            src_ref=loss_out,
            dst_ref=loss_in.at[i],
            send_sem=loss_send.at[i],
            recv_sem=loss_recv.at[i],
            device_id=(lax.rem(dp + i, N_DP), me),
            device_id_type=MESH,
        )
        copy.start()
        lefts.append(copy)
    slot = lax.broadcasted_iota(jnp.int32, (CLIPS, HEAD_DIM), 0)
    scores = jnp.where(slot + dp * CLIPS == order_lane, losses, 0.0)
    for i in range(1, N_DP):
        lefts[i - 1].wait_recv()
        group = lax.rem(dp - i + N_DP, N_DP)
        scores = scores + jnp.where(slot + group * CLIPS == order_lane, loss_in[i], 0.0)
    out_ref[...] = jnp.sum(scores, axis=0, keepdims=True)

    for row in sends:
        for copy in row:
            copy.wait_send()
    for peer in peers:
        message_copy(peer).wait_send()
    for copy in parts:
        copy.wait_send()
    for copy in lefts:
        copy.wait_send()


def per_device(
    queries, keys, values, text_kv, text_lengths, clip_lengths, timesteps, mod_weight, final_weight, noise, clean, report_order
):
    activated = jax.nn.silu(step_embedding(timesteps)).astype(BF16)
    text = text_kv.reshape(CLIPS, 2 * TEXT, HEAD_DIM)
    anywhere = pl.BlockSpec(memory_space=pl.ANY)
    vmem = pl.BlockSpec(memory_space=pltpu.VMEM)
    smem = pl.BlockSpec(memory_space=pltpu.SMEM)
    dma = pltpu.SemaphoreType.DMA
    out = pl.pallas_call(
        kernel,
        out_shape=jax.ShapeDtypeStruct((1, HEAD_DIM), F32),
        in_specs=[anywhere] * 4 + [vmem] + [smem] * 3 + [anywhere] * 4,
        out_specs=vmem,
        scratch_shapes=[
            pltpu.VMEM((ROWS, HEAD_DIM), BF16),
            pltpu.VMEM((ROWS + 2 * PAD, HEAD_DIM), BF16),
            pltpu.VMEM((ROWS + 2 * PAD, HEAD_DIM), BF16),
            pltpu.VMEM((CLIPS, 2 * TEXT, HEAD_DIM), BF16),
            pltpu.VMEM((FREQ, 2 * WIDTH), BF16),
            pltpu.VMEM((CHANNELS, WIDTH), BF16),
            pltpu.VMEM((CHANNELS, TOK), F32),
            pltpu.VMEM((CHANNELS, TOK), F32),
            pltpu.VMEM((CLIPS * TEXT, HEAD_DIM), BF16),
            pltpu.VMEM((CLIPS * TEXT, HEAD_DIM), BF16),
            pltpu.VMEM((ROWS, HEAD_DIM), BF16),
            pltpu.VMEM((ROWS + 2 * PAD, HEAD_DIM), BF16),
            pltpu.VMEM((CLIPS * TEXT, HEAD_DIM), BF16),
            pltpu.VMEM((CLIPS, ROWS), F32),
            pltpu.VMEM((CLIPS, ROWS), jnp.int32),
            pltpu.VMEM((CLIPS * CHANNELS, 2 * HEAD_DIM), BF16),
            pltpu.VMEM((CHANNELS, TOK), F32),
            pltpu.VMEM((CHANNELS, TOK), F32),
            pltpu.VMEM((CHANNELS, TOK), F32),
            pltpu.VMEM((ROWS, HEAD_DIM), F32),
            pltpu.VMEM((ROWS, HEAD_DIM), F32),
            pltpu.VMEM((ROWS, HEAD_DIM), F32),
            pltpu.VMEM((ROWS, HEAD_DIM), F32),
            pltpu.VMEM((ROWS, WINDOW), BF16),
            pltpu.VMEM((N_SEQ, MSG, TOK), BF16),
            pltpu.VMEM((N_SEQ, MSG, TOK), BF16),
            pltpu.VMEM((CLIPS, HEAD_DIM), F32),
            pltpu.VMEM((N_SEQ, CLIPS, HEAD_DIM), F32),
            pltpu.VMEM((CLIPS, HEAD_DIM), F32),
            pltpu.VMEM((N_DP, CLIPS, HEAD_DIM), F32),
            dma((3, N_SEQ)),
            dma((3, N_SEQ)),
            dma((3,)),
            dma((5,)),
            dma((N_SEQ,)),
            dma((N_SEQ,)),
            dma((N_SEQ,)),
            dma((N_SEQ,)),
            dma((N_DP,)),
            dma((N_DP,)),
        ],
        compiler_params=pltpu.CompilerParams(
            collective_id=0, has_side_effects=True, vmem_limit_bytes=60 * 1024 * 1024
        ),
    )(
        queries, keys, values, text, activated, text_lengths, clip_lengths, report_order, mod_weight, final_weight.T, noise.T, clean.T
    )
    return out[0, :CLIPS]


def solution(mesh):
    rows = P(("dp", "seq"), None)
    in_specs = (
        rows, rows, rows, P("dp", None, None, "seq"), P("dp"), P("dp", None), P("dp"), P(), P(), rows, rows, P("dp"),
    )
    return jax.shard_map(per_device, mesh=mesh, in_specs=in_specs, out_specs=P("dp"), check_vma=False)
```

```python
import functools
import math

import jax
import jax.numpy as jnp
from jax import lax
from jax.experimental import pallas as pl
from jax.experimental.pallas import tpu as pltpu
from jax.sharding import PartitionSpec as P

MESH = pl.DeviceIdType.MESH
HEAD_DIM = 128
FREQ = 256
CLIPS = 8
TEXT = 256
CHANNELS = 64
WIDTH = 2048
TOK = 128
N_SEQ = 16
N_DP = 32
ROWS = TOK * N_SEQ
BLOCK = 256
BLOCKS = ROWS // BLOCK
PAD = 512
WINDOW = BLOCK + 2 * PAD
NEAR_CLIPS = 5
SPAN = NEAR_CLIPS * TEXT
MSG = 80
FAR = 65536.0
EPS = 1e-06
SCALE = math.log2(math.e) / math.sqrt(HEAD_DIM)
NT = (((1,), (1,)), ((), ()))
F32 = jnp.float32
BF16 = jnp.bfloat16


def nt_dot(a, b):
    return lax.dot_general(a, b, NT, preferred_element_type=F32)


def nn_dot(a, b):
    return jnp.dot(a, b, preferred_element_type=F32)


def pieces(x, count):
    out = []
    for _ in range(count):
        piece = x.astype(BF16)
        out.append(piece)
        x = x - piece.astype(F32)
    return out


def along(scalars, shape, dim):
    place = lax.broadcasted_iota(jnp.int32, shape, dim)
    out = jnp.zeros(shape, jnp.int32)
    for index, scalar in enumerate(scalars):
        out = jnp.where(place == index, scalar, out)
    return out


PARTNERS = [(0, 1), (1, 0), (-1, 0), (1, 1), (-1, 1), (2, 0), (-2, 0), (2, 1), (-2, 1)]
PARTNERS += [(3, 0), (-3, 0), (3, 1), (-3, 1), (4, 0), (4, 1)]


def wait_for(buffer, sem):
    pltpu.make_async_copy(buffer, buffer, sem).wait()


def kernel(
    q_hbm, k_hbm, v_hbm, text_hbm, tlen_hbm, clen_hbm, order_hbm, time_hbm, modw_hbm, finw_hbm, noise_hbm, clean_hbm,
    out_ref,
    qbuf, kbuf, vbuf, textbuf, modw, finw, noise, clean, tlen_ref, clen_ref, order_ref, time_ref,
    tk, tv, qbias, kbias, tbias, onehot, clip_row, wall, btok, ctok, target,
    text_max, text_sum, text_out, inverse, weights, message, gathered, part_out, part_in, loss_out, loss_in,
    load_sem, in_send, in_recv, msg_send, msg_recv, part_send, part_recv, loss_send, loss_recv,
):
    me = lax.axis_index("seq")
    dp = lax.axis_index("dp")
    z = me // 2
    core = me % 2
    peers = [lax.rem(z + dz + 8, 8) * 2 + lax.rem(core + dc, 2) for dz, dc in PARTNERS]

    barrier = pltpu.get_barrier_semaphore()
    for peer in peers:
        pl.semaphore_signal(barrier, inc=1, device_id=(dp, peer), device_id_type=MESH)
    for i in range(1, N_DP):
        pl.semaphore_signal(barrier, inc=1, device_id=(lax.rem(dp + i, N_DP), me), device_id_type=MESH)

    loads = [
        pltpu.make_async_copy(src, dst, load_sem.at[i])
        for i, (src, dst) in enumerate(
            [
                (tlen_hbm, tlen_ref), (clen_hbm, clen_ref), (order_hbm, order_ref), (time_hbm, time_ref),
                (text_hbm, textbuf), (modw_hbm, modw), (finw_hbm, finw), (noise_hbm, noise), (clean_hbm, clean),
            ]
        )
    ]
    for load in loads:
        load.start()
    head_at = pl.multiple_of(me * HEAD_DIM, HEAD_DIM)
    streams = [(q_hbm, qbuf, 0), (k_hbm, kbuf, PAD), (v_hbm, vbuf, PAD)]
    for t, (src, dst, base) in enumerate(streams):
        pltpu.make_async_copy(
            src.at[:, pl.ds(head_at, HEAD_DIM)], dst.at[pl.ds(pl.multiple_of(base + me * TOK, TOK), TOK)], in_recv.at[t]
        ).start()

    pl.semaphore_wait(barrier, N_SEQ - 1 + N_DP - 1)

    for t, (src, dst, base) in enumerate(streams):
        for peer in reversed(peers):
            pltpu.make_async_remote_copy(
                src_ref=src.at[:, pl.ds(pl.multiple_of(peer * HEAD_DIM, HEAD_DIM), HEAD_DIM)],
                dst_ref=dst.at[pl.ds(pl.multiple_of(base + me * TOK, TOK), TOK)],
                send_sem=in_send.at[t],
                recv_sem=in_recv.at[t],
                device_id=(dp, peer),
                device_id_type=MESH,
            ).start()
    for load in loads[:4]:
        load.wait()

    starts, ends = [], []
    total = jnp.int32(0)
    for c in range(CLIPS):
        starts.append(total)
        total = total + clen_ref[0, c]
        ends.append(total)
    start_lane, end_lane = along(starts, (1, HEAD_DIM), 1), along(ends, (1, HEAD_DIM), 1)
    start_col, end_col = along(starts, (CLIPS, 1), 0), along(ends, (CLIPS, 1), 0)
    size_row = jnp.where(end_lane > start_lane, end_lane - start_lane, 1).astype(F32)
    place = lax.broadcasted_iota(jnp.int32, (CLIPS, ROWS), 1)
    onehot[...] = jnp.where((place >= start_col) & (place < end_col), 1.0, 0.0)
    clip_of = jnp.zeros((CLIPS, ROWS), jnp.int32)
    for c in range(1, CLIPS):
        clip_of = clip_of + jnp.where(place >= starts[c], 1, 0)
    clip_row[...] = clip_of
    edge = jnp.zeros((PAD, HEAD_DIM), BF16)
    for buf in (kbuf, vbuf):
        buf[pl.ds(0, PAD), :] = edge
        buf[pl.ds(PAD + ROWS, PAD), :] = edge

    rows_iota = lax.broadcasted_iota(jnp.int32, (BLOCK, HEAD_DIM), 0)
    lane_iota = lax.broadcasted_iota(jnp.int32, (BLOCK, HEAD_DIM), 1)

    def fill_key_bias(i, _):
        token = rows_iota + (i * BLOCK - PAD)
        live = (token >= start_lane) & (token < end_lane)
        kbias[pl.ds(pl.multiple_of(i * BLOCK, BLOCK), BLOCK), :] = jnp.where(live, 0.0, -FAR).astype(BF16)
        return 0

    def fill_query_bias(i, _):
        token = rows_iota + i * BLOCK
        live = (token >= start_lane) & (token < end_lane)
        qbias[pl.ds(pl.multiple_of(i * BLOCK, BLOCK), BLOCK), :] = jnp.where(live, 1.0, 0.0).astype(BF16)
        return 0

    lax.fori_loop(0, (ROWS + 2 * PAD) // BLOCK, fill_key_bias, 0)
    lax.fori_loop(0, BLOCKS, fill_query_bias, 0)

    loads[4].wait()
    sub = lax.broadcasted_iota(jnp.int32, (TEXT, 2 * TEXT), 0)
    lane = lax.broadcasted_iota(jnp.int32, (TEXT, 2 * TEXT), 1)
    pick_key = jnp.where(lane == 2 * sub, 1.0, 0.0).astype(BF16)
    pick_value = jnp.where(lane == 2 * sub + 1, 1.0, 0.0).astype(BF16)
    length_lane = along([tlen_ref[c] for c in range(CLIPS)], (1, HEAD_DIM), 1)

    def split_text(c, _):
        both = textbuf[c]
        rows = pl.ds(pl.multiple_of(c * TEXT, TEXT), TEXT)
        tk[rows, :] = nn_dot(pick_key, both).astype(BF16)
        tv[rows, :] = nn_dot(pick_value, both).astype(BF16)
        live = (lane_iota == c) & (rows_iota < length_lane)
        tbias[rows, :] = jnp.where(live, 0.0, -FAR).astype(BF16)
        return 0

    lax.fori_loop(0, CLIPS, split_text, 0)

    loads[5].wait()
    loads[6].wait()
    step = along([time_ref[c] for c in range(CLIPS)], (CLIPS, FREQ // 2), 0).astype(F32)
    ramp = lax.broadcasted_iota(jnp.int32, (CLIPS, FREQ // 2), 1).astype(F32)
    angles = step * jnp.exp(-math.log(10000.0) * ramp / (FREQ // 2))
    embedding = jnp.concatenate([jnp.cos(angles), jnp.sin(angles)], axis=1)
    act = jax.nn.silu(embedding).astype(BF16)
    gain = 1.0 + nn_dot(act, modw[:, pl.ds(WIDTH + head_at, HEAD_DIM)])
    turned = finw[:, pl.ds(head_at, HEAD_DIM)].astype(F32)
    for c in range(CLIPS):
        high, low = pieces(turned * gain[c : c + 1, :], 2)
        wall[pl.ds(c * CHANNELS, CHANNELS), :] = jnp.concatenate([high, low], axis=1)
    shift_all = nn_dot(act, modw[:, pl.ds(0, WIDTH)])
    gain_all = 1.0 + nn_dot(act, modw[:, pl.ds(WIDTH, WIDTH)])
    stacked = jnp.concatenate(pieces(gain_all, 3) + pieces(shift_all, 3), axis=0)
    folded = nt_dot(finw[...], stacked)
    gain_sum = folded[:, 0:8] + folded[:, 8:16] + folded[:, 16:24]
    shift_sum = folded[:, 24:32] + folded[:, 32:40] + folded[:, 40:48]
    mine = onehot[:, pl.ds(pl.multiple_of(me * TOK, TOK), TOK)]
    gain_tok = jnp.zeros((CHANNELS, TOK), F32)
    shift_tok = jnp.zeros((CHANNELS, TOK), F32)
    for c in range(CLIPS):
        gain_tok = gain_tok + gain_sum[:, c : c + 1] * mine[c : c + 1, :]
        shift_tok = shift_tok + shift_sum[:, c : c + 1] * mine[c : c + 1, :]
    btok[...] = gain_tok
    ctok[...] = shift_tok
    loads[7].wait()
    loads[8].wait()
    target[...] = noise[...] - clean[...]
    order_col = along([order_ref[c] for c in range(CLIPS)], (CLIPS, HEAD_DIM), 0)
    order_lane = lax.broadcasted_iota(jnp.int32, (CLIPS, HEAD_DIM), 1)
    wanted = jnp.where(order_lane < CLIPS, order_col - order_lane, -1)

    wait_for(qbuf, in_recv.at[0])
    one_lanes = jnp.ones((SPAN, HEAD_DIM), BF16)

    def text_block(b, _):
        rows = pl.ds(pl.multiple_of(b * BLOCK, BLOCK), BLOCK)
        span = pl.ds(pl.multiple_of(b // 2 * TEXT, TEXT), SPAN)
        left = jnp.concatenate([qbuf[rows, :], qbias[rows, :]], axis=1)
        right = jnp.concatenate([tk[span, :], tbias[span, :]], axis=1)
        scores = nt_dot(left, right)
        top = jnp.max(scores, axis=1, keepdims=True)
        weight = jnp.exp2((scores - top) * SCALE).astype(BF16)
        mixed = nn_dot(weight, jnp.concatenate([tv[span, :], one_lanes], axis=1))
        text_max[rows, :] = jnp.broadcast_to(top, (BLOCK, HEAD_DIM))
        text_out[rows, :] = mixed[:, :HEAD_DIM]
        text_sum[rows, :] = mixed[:, HEAD_DIM:]
        return 0

    lax.fori_loop(0, BLOCKS, text_block, 0)

    wait_for(kbuf.at[pl.ds(PAD, ROWS)], in_recv.at[1])
    one_wide = jnp.ones((WINDOW, HEAD_DIM), BF16)

    def score_block(b, _):
        rows = pl.ds(pl.multiple_of(b * BLOCK, BLOCK), BLOCK)
        window = pl.ds(pl.multiple_of(b * BLOCK, BLOCK), WINDOW)
        left = jnp.concatenate([qbuf[rows, :], qbias[rows, :]], axis=1)
        right = jnp.concatenate([kbuf[window, :], kbias[window, :]], axis=1)
        scores = nt_dot(left, right)
        before = text_max[rows, :]
        top = jnp.maximum(before, jnp.max(scores, axis=1, keepdims=True))
        weight = jnp.exp2((scores - top[:, :1]) * SCALE).astype(BF16)
        weights[rows, :] = weight
        fade = jnp.exp2((before - top) * SCALE)
        inv = 1.0 / (nn_dot(weight, one_wide) + text_sum[rows, :] * fade)
        inverse[rows, :] = inv
        text_out[rows, :] = text_out[rows, :] * (fade * inv)
        return 0

    lax.fori_loop(0, BLOCKS, score_block, 0)

    wait_for(vbuf.at[pl.ds(PAD, ROWS)], in_recv.at[2])
    ones_row = jnp.ones((8, 2 * HEAD_DIM), BF16)
    row8 = lax.broadcasted_iota(jnp.int32, (8, TOK), 0)

    def value_block(i, _):
        reach = (i + 1) // 2
        step = 4 + reach - 2 * reach * lax.rem(i, 2)
        b = lax.rem(z + step, 8)
        rows = pl.ds(pl.multiple_of(b * BLOCK, BLOCK), BLOCK)
        window = pl.ds(pl.multiple_of(b * BLOCK, BLOCK), WINDOW)
        first = b // 2
        mixed = nn_dot(weights[rows, :], vbuf[window, :])
        attended = (mixed * inverse[rows, :] + text_out[rows, :]).astype(BF16)
        fold = wall[pl.ds(pl.multiple_of(first * CHANNELS, CHANNELS), NEAR_CLIPS * CHANNELS), :]
        for half in range(2):
            owner = 2 * b + half
            part = attended[half * TOK : (half + 1) * TOK]
            spread = nt_dot(fold, jnp.concatenate([part, part], axis=1))
            picked = jnp.zeros((CHANNELS, TOK), F32)
            clip_here = clip_row[0:1, pl.ds(pl.multiple_of(owner * TOK, TOK), TOK)]
            for j in range(NEAR_CLIPS):
                picked = jnp.where(clip_here == first + j, spread[j * CHANNELS : (j + 1) * CHANNELS], picked)
            wide_part = part.astype(F32)
            total = nt_dot(ones_row[:, :HEAD_DIM], part)
            squares = nt_dot(ones_row, jnp.concatenate(pieces(wide_part * wide_part, 2), axis=1))
            total_high, total_low = [x.astype(F32) for x in pieces(total, 2)]
            square_high, square_low = [x.astype(F32) for x in pieces(squares, 2)]
            stats = jnp.where(row8 == 0, total_high, jnp.where(row8 == 1, total_low, jnp.where(row8 == 2, square_high, square_low)))
            message[owner] = jnp.concatenate([picked, stats, jnp.zeros((8, TOK), F32)], axis=0).astype(BF16)

            @pl.when(owner != me)
            def _():
                pltpu.make_async_remote_copy(
                    src_ref=message.at[owner],
                    dst_ref=gathered.at[me],
                    send_sem=msg_send.at[0],
                    recv_sem=msg_recv.at[0],
                    device_id=(dp, owner),
                    device_id_type=MESH,
                ).start()

        return 0

    lax.fori_loop(0, BLOCKS, value_block, 0)

    pltpu.make_async_copy(message.at[me], gathered.at[me], msg_recv.at[0]).start()
    wait_for(gathered, msg_recv.at[0])
    total = jnp.zeros((MSG, TOK), F32)
    for head in range(N_SEQ):
        total = total + gathered[head].astype(F32)
    center = (total[64:65] + total[65:66]) / WIDTH
    spread = (total[66:67] + total[67:68]) / WIDTH - center * center
    predicted = lax.rsqrt(spread + EPS) * (total[:CHANNELS] - center * btok[...]) + ctok[...]
    difference = predicted - target[...]
    error = jnp.sum(difference * difference, axis=0, keepdims=True) / CHANNELS
    mine = onehot[:, pl.ds(pl.multiple_of(me * TOK, TOK), TOK)]
    slot = lax.broadcasted_iota(jnp.int32, (CLIPS, HEAD_DIM), 0)
    lanes = lax.broadcasted_iota(jnp.int32, (CLIPS, HEAD_DIM), 1)
    partial = jnp.sum(mine * error, axis=1, keepdims=True)
    partial = jnp.sum(jnp.where(slot == lanes, partial, 0.0), axis=0, keepdims=True)
    part_out[...] = partial
    for peer in reversed(peers):
        pltpu.make_async_remote_copy(
            src_ref=part_out,
            dst_ref=part_in.at[me],
            send_sem=part_send.at[0],
            recv_sem=part_recv.at[0],
            device_id=(dp, peer),
            device_id_type=MESH,
        ).start()
    part_in[me] = partial
    wait_for(part_in.at[pl.ds(0, N_SEQ - 1)], part_recv.at[0])
    partial = part_in[0]
    for rank in range(1, N_SEQ):
        partial = partial + part_in[rank]
    losses = partial / size_row
    loss_out[...] = losses
    for i in range(1, N_DP):
        pltpu.make_async_remote_copy(
            src_ref=loss_out,
            dst_ref=loss_in.at[dp],
            send_sem=loss_send.at[0],
            recv_sem=loss_recv.at[0],
            device_id=(lax.rem(dp + i, N_DP), me),
            device_id_type=MESH,
        ).start()
    loss_in[dp] = losses
    wait_for(loss_in.at[pl.ds(0, N_DP - 1)], loss_recv.at[0])
    scores = jnp.zeros((CLIPS, HEAD_DIM), F32)
    for group in range(N_DP):
        scores = scores + jnp.where(wanted == group * CLIPS, loss_in[group], 0.0)
    scores = jnp.sum(scores, axis=1, keepdims=True)
    out_ref[...] = jnp.sum(jnp.where(slot == lanes, scores, 0.0), axis=0, keepdims=True)

    for t in range(3):
        wait_for(qbuf.at[pl.ds(0, (N_SEQ - 1) * TOK)], in_send.at[t])
    wait_for(message.at[pl.ds(0, N_SEQ - 1)], msg_send.at[0])
    wait_for(part_in.at[pl.ds(0, N_SEQ - 1)], part_send.at[0])
    wait_for(loss_in.at[pl.ds(0, N_DP - 1)], loss_send.at[0])


def per_device(
    queries, keys, values, text_kv, text_lengths, clip_lengths, timesteps, mod_weight, final_weight, noise, clean, report_order
):
    text = text_kv.reshape(CLIPS, 2 * TEXT, HEAD_DIM)
    anywhere = pl.BlockSpec(memory_space=pl.ANY)
    vmem = pl.BlockSpec(memory_space=pltpu.VMEM)
    dma = pltpu.SemaphoreType.DMA
    out = pl.pallas_call(
        kernel,
        out_shape=jax.ShapeDtypeStruct((1, HEAD_DIM), F32),
        in_specs=[anywhere] * 12,
        out_specs=vmem,
        scratch_shapes=[
            pltpu.VMEM((ROWS, HEAD_DIM), BF16),
            pltpu.VMEM((ROWS + 2 * PAD, HEAD_DIM), BF16),
            pltpu.VMEM((ROWS + 2 * PAD, HEAD_DIM), BF16),
            pltpu.VMEM((CLIPS, 2 * TEXT, HEAD_DIM), BF16),
            pltpu.VMEM((FREQ, 2 * WIDTH), BF16),
            pltpu.VMEM((CHANNELS, WIDTH), BF16),
            pltpu.VMEM((CHANNELS, TOK), F32),
            pltpu.VMEM((CHANNELS, TOK), F32),
            pltpu.SMEM((CLIPS,), jnp.int32),
            pltpu.SMEM((1, CLIPS), jnp.int32),
            pltpu.SMEM((CLIPS,), jnp.int32),
            pltpu.SMEM((CLIPS,), jnp.int32),
            pltpu.VMEM((CLIPS * TEXT, HEAD_DIM), BF16),
            pltpu.VMEM((CLIPS * TEXT, HEAD_DIM), BF16),
            pltpu.VMEM((ROWS, HEAD_DIM), BF16),
            pltpu.VMEM((ROWS + 2 * PAD, HEAD_DIM), BF16),
            pltpu.VMEM((CLIPS * TEXT, HEAD_DIM), BF16),
            pltpu.VMEM((CLIPS, ROWS), F32),
            pltpu.VMEM((CLIPS, ROWS), jnp.int32),
            pltpu.VMEM((CLIPS * CHANNELS, 2 * HEAD_DIM), BF16),
            pltpu.VMEM((CHANNELS, TOK), F32),
            pltpu.VMEM((CHANNELS, TOK), F32),
            pltpu.VMEM((CHANNELS, TOK), F32),
            pltpu.VMEM((ROWS, HEAD_DIM), F32),
            pltpu.VMEM((ROWS, HEAD_DIM), F32),
            pltpu.VMEM((ROWS, HEAD_DIM), F32),
            pltpu.VMEM((ROWS, HEAD_DIM), F32),
            pltpu.VMEM((ROWS, WINDOW), BF16),
            pltpu.VMEM((N_SEQ, MSG, TOK), BF16),
            pltpu.VMEM((N_SEQ, MSG, TOK), BF16),
            pltpu.VMEM((1, HEAD_DIM), F32),
            pltpu.VMEM((N_SEQ, 1, HEAD_DIM), F32),
            pltpu.VMEM((1, HEAD_DIM), F32),
            pltpu.VMEM((N_DP, 1, HEAD_DIM), F32),
            dma((9,)),
            dma((3,)),
            dma((3,)),
            dma((1,)),
            dma((1,)),
            dma((1,)),
            dma((1,)),
            dma((1,)),
            dma((1,)),
        ],
        compiler_params=pltpu.CompilerParams(
            collective_id=0, has_side_effects=True, vmem_limit_bytes=60 * 1024 * 1024
        ),
    )(
        queries, keys, values, text, text_lengths, clip_lengths, report_order, timesteps, mod_weight, final_weight.T, noise.T, clean.T
    )
    return out[0, :CLIPS]


def solution(mesh):
    rows = P(("dp", "seq"), None)
    in_specs = (
        rows, rows, rows, P("dp", None, None, "seq"), P("dp"), P("dp", None), P("dp"), P(), P(), rows, rows, P("dp"),
    )
    return jax.shard_map(per_device, mesh=mesh, in_specs=in_specs, out_specs=P("dp"), check_vma=False)
```

```python
import functools
import math

import jax
import jax.numpy as jnp
from jax import lax
from jax.experimental import pallas as pl
from jax.experimental.pallas import tpu as pltpu
from jax.sharding import PartitionSpec as P

MESH = pl.DeviceIdType.MESH
HEAD_DIM = 128
FREQ = 256
CLIPS = 8
TEXT = 256
CHANNELS = 64
WIDTH = 2048
TOK = 128
N_SEQ = 16
N_DP = 32
ROWS = TOK * N_SEQ
BLOCK = 256
BLOCKS = ROWS // BLOCK
PAD = 512
WINDOW = BLOCK + 2 * PAD
NEAR_CLIPS = 5
SPAN = NEAR_CLIPS * TEXT
MSG = 80
FAR = 65536.0
EPS = 1e-06
SCALE = math.log2(math.e) / math.sqrt(HEAD_DIM)
NT = (((1,), (1,)), ((), ()))
F32 = jnp.float32
BF16 = jnp.bfloat16


def nt_dot(a, b):
    return lax.dot_general(a, b, NT, preferred_element_type=F32)


def nn_dot(a, b):
    return jnp.dot(a, b, preferred_element_type=F32)


def pieces(x, count):
    out = []
    for _ in range(count):
        piece = x.astype(BF16)
        out.append(piece)
        x = x - piece.astype(F32)
    return out


def along(scalars, shape, dim):
    place = lax.broadcasted_iota(jnp.int32, shape, dim)
    out = jnp.zeros(shape, jnp.int32)
    for index, scalar in enumerate(scalars):
        out = jnp.where(place == index, scalar, out)
    return out


PARTNERS = [(0, 1), (1, 0), (-1, 0), (1, 1), (-1, 1), (2, 0), (-2, 0), (2, 1), (-2, 1)]
NEAR = len(PARTNERS)
PARTNERS += [(3, 0), (-3, 0), (3, 1), (-3, 1), (4, 0), (4, 1)]


GROUPS = sorted(
    [(dx, dy) for dx in range(4) for dy in range(8) if dx or dy],
    key=lambda step: -(min(step[0], 4 - step[0]) + min(step[1], 8 - step[1])),
)
SOURCES = [0, 4, 3, -3, 2, -2, 1, -1]
EARLY = 6
FINISH = [4, 3, -3, 2, -2, 1, -1, 0]


def wait_for(buffer, sem):
    pltpu.make_async_copy(buffer, buffer, sem).wait()


def kernel(
    q_hbm, k_hbm, v_hbm, text_hbm, tlen_hbm, clen_hbm, order_hbm, time_hbm, modw_hbm, finw_hbm, noise_hbm, clean_hbm,
    out_ref,
    qbuf, kbuf, vbuf, textbuf, modw, finw, noise, clean, tlen_ref, clen_ref, order_ref, time_ref,
    tk, tv, qbias, kbias, tbias, onehot, clip_row, wall, btok, ctok, target,
    text_max, text_sum, text_out, inverse, weights, mixed_out, pair, taken, message, gathered, part_out, part_in, loss_out, loss_in,
    far_sem, cross_sem, load_sem, in_send, in_recv, value_recv, pair_send, pair_recv, msg_send, msg_recv, part_send, part_recv, loss_send, loss_recv,
):
    me = lax.axis_index("seq")
    dp = lax.axis_index("dp")
    z = me // 2
    core = me % 2
    peers = [lax.rem(z + dz + 8, 8) * 2 + lax.rem(core + dc, 2) for dz, dc in PARTNERS]

    barrier = pltpu.get_barrier_semaphore()
    for peer in peers[:NEAR]:
        pl.semaphore_signal(barrier, inc=1, device_id=(dp, peer), device_id_type=MESH)
    across = [lax.rem(dp // 8 + i, 4) * 8 + lax.rem(dp, 8) for i in range(1, 4)]
    down = [dp // 8 * 8 + lax.rem(lax.rem(dp, 8) + i, 8) for i in range(1, 8)]
    for group in across + down:
        pl.semaphore_signal(barrier, inc=1, device_id=(group, me), device_id_type=MESH)

    loads = [
        pltpu.make_async_copy(src, dst, load_sem.at[i])
        for i, (src, dst) in enumerate(
            [
                (tlen_hbm, tlen_ref), (clen_hbm, clen_ref), (order_hbm, order_ref), (time_hbm, time_ref),
                (text_hbm, textbuf), (modw_hbm, modw), (finw_hbm, finw), (noise_hbm, noise), (clean_hbm, clean),
            ]
        )
    ]
    for load in loads:
        load.start()
    head_at = pl.multiple_of(me * HEAD_DIM, HEAD_DIM)
    streams = [(q_hbm, qbuf, 0), (k_hbm, kbuf, PAD), (v_hbm, vbuf, PAD)]
    for t, (src, dst, base) in enumerate(streams):
        pltpu.make_async_copy(
            src.at[:, pl.ds(head_at, HEAD_DIM)],
            dst.at[pl.ds(pl.multiple_of(base + me * TOK, TOK), TOK)],
            in_recv.at[t] if t < 2 else value_recv.at[0],
        ).start()

    pl.semaphore_wait(barrier, NEAR + len(across) + len(down))
    for dz in (2, -2):
        pl.semaphore_signal(far_sem, inc=1, device_id=(dp, lax.rem(z + dz + 8, 8) * 2 + core), device_id_type=MESH)
    for group in across:
        pl.semaphore_signal(cross_sem, inc=1, device_id=(group, me), device_id_type=MESH)

    def send_part(t, partners):
        src, dst, base = streams[t]
        for dz, dc in partners:
            peer = lax.rem(z + dz + 8, 8) * 2 + lax.rem(core + dc, 2)
            pltpu.make_async_remote_copy(
                src_ref=src.at[:, pl.ds(pl.multiple_of(peer * HEAD_DIM, HEAD_DIM), HEAD_DIM)],
                dst_ref=dst.at[pl.ds(pl.multiple_of(base + me * TOK, TOK), TOK)],
                send_sem=in_send.at[t],
                recv_sem=in_recv.at[t] if t < 2 else value_recv.at[dz % 8],
                device_id=(dp, peer),
                device_id_type=MESH,
            ).start()

    send_part(0, PARTNERS[:NEAR][::-1])
    pl.semaphore_wait(far_sem, 2)
    send_part(0, PARTNERS[NEAR:][::-1])
    send_part(1, PARTNERS[::-1])
    send_part(2, PARTNERS[::-1])
    for load in loads[:4]:
        load.wait()

    starts, ends = [], []
    total = jnp.int32(0)
    for c in range(CLIPS):
        starts.append(total)
        total = total + clen_ref[0, c]
        ends.append(total)
    start_lane, end_lane = along(starts, (1, HEAD_DIM), 1), along(ends, (1, HEAD_DIM), 1)
    start_col, end_col = along(starts, (CLIPS, 1), 0), along(ends, (CLIPS, 1), 0)
    size_row = jnp.where(end_lane > start_lane, end_lane - start_lane, 1).astype(F32)
    place = lax.broadcasted_iota(jnp.int32, (CLIPS, ROWS), 1)
    onehot[...] = jnp.where((place >= start_col) & (place < end_col), 1.0, 0.0)
    clip_of = jnp.zeros((CLIPS, ROWS), jnp.int32)
    for c in range(1, CLIPS):
        clip_of = clip_of + jnp.where(place >= starts[c], 1, 0)
    clip_row[...] = clip_of
    edge = jnp.zeros((PAD, HEAD_DIM), BF16)
    for buf in (kbuf, vbuf):
        buf[pl.ds(0, PAD), :] = edge
        buf[pl.ds(PAD + ROWS, PAD), :] = edge

    rows_iota = lax.broadcasted_iota(jnp.int32, (BLOCK, HEAD_DIM), 0)
    lane_iota = lax.broadcasted_iota(jnp.int32, (BLOCK, HEAD_DIM), 1)

    def fill_key_bias(i, _):
        token = rows_iota + (i * BLOCK - PAD)
        live = (token >= start_lane) & (token < end_lane)
        kbias[pl.ds(pl.multiple_of(i * BLOCK, BLOCK), BLOCK), :] = jnp.where(live, 0.0, -FAR).astype(BF16)
        return 0

    def fill_query_bias(i, _):
        token = rows_iota + i * BLOCK
        live = (token >= start_lane) & (token < end_lane)
        qbias[pl.ds(pl.multiple_of(i * BLOCK, BLOCK), BLOCK), :] = jnp.where(live, 1.0, 0.0).astype(BF16)
        return 0

    lax.fori_loop(0, (ROWS + 2 * PAD) // BLOCK, fill_key_bias, 0)
    lax.fori_loop(0, BLOCKS, fill_query_bias, 0)

    loads[4].wait()
    sub = lax.broadcasted_iota(jnp.int32, (TEXT, 2 * TEXT), 0)
    lane = lax.broadcasted_iota(jnp.int32, (TEXT, 2 * TEXT), 1)
    pick_key = jnp.where(lane == 2 * sub, 1.0, 0.0).astype(BF16)
    pick_value = jnp.where(lane == 2 * sub + 1, 1.0, 0.0).astype(BF16)
    length_lane = along([tlen_ref[c] for c in range(CLIPS)], (1, HEAD_DIM), 1)

    def split_text(c, _):
        both = textbuf[c]
        rows = pl.ds(pl.multiple_of(c * TEXT, TEXT), TEXT)
        tk[rows, :] = nn_dot(pick_key, both).astype(BF16)
        tv[rows, :] = nn_dot(pick_value, both).astype(BF16)
        live = (lane_iota == c) & (rows_iota < length_lane)
        tbias[rows, :] = jnp.where(live, 0.0, -FAR).astype(BF16)
        return 0

    lax.fori_loop(0, CLIPS, split_text, 0)

    loads[5].wait()
    loads[6].wait()
    step = along([time_ref[c] for c in range(CLIPS)], (CLIPS, FREQ // 2), 0).astype(F32)
    ramp = lax.broadcasted_iota(jnp.int32, (CLIPS, FREQ // 2), 1).astype(F32)
    angles = step * jnp.exp(-math.log(10000.0) * ramp / (FREQ // 2))
    embedding = jnp.concatenate([jnp.cos(angles), jnp.sin(angles)], axis=1)
    act = jax.nn.silu(embedding).astype(BF16)
    gain = 1.0 + nn_dot(act, modw[:, pl.ds(WIDTH + head_at, HEAD_DIM)])
    turned = finw[:, pl.ds(head_at, HEAD_DIM)].astype(F32)
    for c in range(CLIPS):
        high, low = pieces(turned * gain[c : c + 1, :], 2)
        wall[pl.ds(c * CHANNELS, CHANNELS), :] = jnp.concatenate([high, low], axis=1)
    shift_all = nn_dot(act, modw[:, pl.ds(0, WIDTH)])
    gain_all = 1.0 + nn_dot(act, modw[:, pl.ds(WIDTH, WIDTH)])
    stacked = jnp.concatenate(pieces(gain_all, 3) + pieces(shift_all, 3), axis=0)
    folded = nt_dot(finw[...], stacked)
    gain_sum = folded[:, 0:8] + folded[:, 8:16] + folded[:, 16:24]
    shift_sum = folded[:, 24:32] + folded[:, 32:40] + folded[:, 40:48]
    mine = onehot[:, pl.ds(pl.multiple_of(me * TOK, TOK), TOK)]
    gain_tok = jnp.zeros((CHANNELS, TOK), F32)
    shift_tok = jnp.zeros((CHANNELS, TOK), F32)
    for c in range(CLIPS):
        gain_tok = gain_tok + gain_sum[:, c : c + 1] * mine[c : c + 1, :]
        shift_tok = shift_tok + shift_sum[:, c : c + 1] * mine[c : c + 1, :]
    btok[...] = gain_tok
    ctok[...] = shift_tok
    loads[7].wait()
    loads[8].wait()
    target[...] = noise[...] - clean[...]
    order_col = along([order_ref[c] for c in range(CLIPS)], (CLIPS, HEAD_DIM), 0)
    order_lane = lax.broadcasted_iota(jnp.int32, (CLIPS, HEAD_DIM), 1)
    wanted = jnp.where(order_lane < CLIPS, order_col - order_lane, -1)

    wait_for(qbuf, in_recv.at[0])
    one_lanes = jnp.ones((SPAN, HEAD_DIM), BF16)

    def text_block(b, _):
        rows = pl.ds(pl.multiple_of(b * BLOCK, BLOCK), BLOCK)
        span = pl.ds(pl.multiple_of(b // 2 * TEXT, TEXT), SPAN)
        left = jnp.concatenate([qbuf[rows, :], qbias[rows, :]], axis=1)
        right = jnp.concatenate([tk[span, :], tbias[span, :]], axis=1)
        scores = nt_dot(left, right)
        top = jnp.max(scores, axis=1, keepdims=True)
        weight = jnp.exp2((scores - top) * SCALE).astype(BF16)
        mixed = nn_dot(weight, jnp.concatenate([tv[span, :], one_lanes], axis=1))
        text_max[rows, :] = jnp.broadcast_to(top, (BLOCK, HEAD_DIM))
        text_out[rows, :] = mixed[:, :HEAD_DIM]
        text_sum[rows, :] = mixed[:, HEAD_DIM:]
        return 0

    lax.fori_loop(0, BLOCKS, text_block, 0)

    wait_for(kbuf.at[pl.ds(PAD, ROWS)], in_recv.at[1])

    def score_block(b, _):
        rows = pl.ds(pl.multiple_of(b * BLOCK, BLOCK), BLOCK)
        window = pl.ds(pl.multiple_of(b * BLOCK, BLOCK), WINDOW)
        left = jnp.concatenate([qbuf[rows, :], qbias[rows, :]], axis=1)
        right = jnp.concatenate([kbuf[window, :], kbias[window, :]], axis=1)
        scores = nt_dot(left, right)
        before = text_max[rows, :]
        top = jnp.maximum(before, jnp.max(scores, axis=1, keepdims=True))
        weight = jnp.exp2((scores - top[:, :1]) * SCALE)
        video_sum = jnp.sum(weight, axis=1, keepdims=True)
        weight = weight.astype(BF16)
        for t in range(5):
            weights[b + t, pl.ds((4 - t) * BLOCK, BLOCK), :] = weight[:, t * BLOCK : (t + 1) * BLOCK]
        fade = jnp.exp2((before - top) * SCALE)
        inv = 1.0 / (video_sum + text_sum[rows, :] * fade)
        inverse[rows, :] = inv
        text_out[rows, :] = text_out[rows, :] * (fade * inv)
        return 0

    lax.fori_loop(0, BLOCKS, score_block, 0, unroll=2)

    mixed_out[...] = jnp.zeros(mixed_out.shape, F32)

    def value_rows(dz):
        chip = lax.rem(z - dz + 8, 8)
        wait_for(vbuf.at[pl.ds(PAD, BLOCK)], value_recv.at[dz % 8])
        return chip, vbuf[pl.ds(pl.multiple_of(PAD + chip * BLOCK, BLOCK), BLOCK), :]

    def add_source(dz):
        chip, rows = value_rows(dz)
        around = pl.ds(pl.multiple_of(chip * BLOCK, BLOCK), 5 * BLOCK)
        mixed_out[around, :] = mixed_out[around, :] + nn_dot(weights[chip + 2], rows)

    ones_rows = jnp.ones((16, HEAD_DIM), BF16)
    zero_rows = jnp.zeros((16, HEAD_DIM), BF16)
    count_left = jnp.concatenate([ones_rows, zero_rows], axis=1)
    count_both = jnp.concatenate([ones_rows, ones_rows], axis=1)
    row16 = lax.broadcasted_iota(jnp.int32, (16, TOK), 0)
    wide16 = lax.broadcasted_iota(jnp.int32, (16, BLOCK), 0)

    def stat_rows(place, total, squares):
        total_high, total_low = [x.astype(F32) for x in pieces(total, 2)]
        square_high, square_low = [x.astype(F32) for x in pieces(squares, 2)]
        rows = jnp.where(place == 2, square_high, jnp.where(place == 3, square_low, 0.0))
        return jnp.where(place == 0, total_high, jnp.where(place == 1, total_low, rows))

    def project(b):
        rows = pl.ds(pl.multiple_of(b * BLOCK, BLOCK), BLOCK)
        first = b // 2
        mixed = mixed_out[pl.ds(pl.multiple_of((b + 2) * BLOCK, BLOCK), BLOCK), :]
        attended = (mixed * inverse[rows, :] + text_out[rows, :]).astype(BF16)
        fold = wall[pl.ds(pl.multiple_of(first * CHANNELS, CHANNELS), NEAR_CLIPS * CHANNELS), :]
        spread = nt_dot(jnp.concatenate([fold, count_left], axis=0), jnp.concatenate([attended, attended], axis=1))
        clip_here = clip_row[0:1, rows]
        picked = spread[:CHANNELS]
        for j in range(1, NEAR_CLIPS):
            picked = jnp.where(clip_here == first + j, spread[j * CHANNELS : (j + 1) * CHANNELS], picked)
        wide = attended.astype(F32)
        squares = nt_dot(count_both, jnp.concatenate(pieces(wide * wide, 2), axis=1))
        stats = stat_rows(wide16, spread[NEAR_CLIPS * CHANNELS :], squares)
        full = jnp.concatenate([picked, stats], axis=0).astype(BF16)
        pair[b, 0] = full[:, :TOK]
        pair[b, 1] = full[:, TOK:]

    def exchange(i, b):
        copy = pltpu.make_async_remote_copy(
            src_ref=pair.at[b, 1 - core],
            dst_ref=taken.at[b],
            send_sem=pair_send.at[0],
            recv_sem=pair_recv.at[i],
            device_id=(dp, z * 2 + 1 - core),
            device_id_type=MESH,
        )
        copy.start()
        return copy

    def message_copy(source, slot, owner):
        pltpu.make_async_remote_copy(
            src_ref=source,
            dst_ref=gathered.at[slot],
            send_sem=msg_send.at[0],
            recv_sem=msg_recv.at[0],
            device_id=(dp, owner),
            device_id_type=MESH,
        ).start()

    def deliver(i, b, copy):
        copy.wait_recv()
        both = pair[b, core].astype(F32) + taken[b].astype(F32)
        stats = stat_rows(row16, both[64:65] + both[65:66], both[66:67] + both[67:68])
        total = jnp.concatenate([both[:CHANNELS], stats], axis=0).astype(BF16)
        if FINISH[i] == 0:
            gathered[2 * z] = total
            return
        message[b] = total
        message_copy(message.at[b], 2 * z, b * 2 + core)

    def finish(i):
        b = lax.rem(z + FINISH[i] + 8, 8)
        project(b)
        if abs(FINISH[i]) == 3:
            for to in range(2):
                message_copy(pair.at[b, to], me, b * 2 + to)
            return None
        return i, b, exchange(i, b)

    for dz in SOURCES[:EARLY]:
        add_source(dz)
    waiting = [finish(0)]
    for dz in SOURCES[EARLY:]:
        add_source(dz)
    for i in range(1, len(FINISH)):
        waiting.append(finish(i))
    for entry in waiting:
        if entry is not None:
            deliver(*entry)

    wait_for(gathered.at[pl.ds(0, 9)], msg_recv.at[0])
    total = gathered[2 * z].astype(F32)
    for dz in (1, 2, 3, 4, 5, 6, 7):
        chip = lax.rem(z + dz, 8)
        total = total + gathered[2 * chip].astype(F32)
        if dz in (3, 5):
            total = total + gathered[2 * chip + 1].astype(F32)
    center = (total[64:65] + total[65:66]) / WIDTH
    spread = (total[66:67] + total[67:68]) / WIDTH - center * center
    predicted = lax.rsqrt(spread + EPS) * (total[:CHANNELS] - center * btok[...]) + ctok[...]
    difference = predicted - target[...]
    error = jnp.sum(difference * difference, axis=0, keepdims=True) / CHANNELS
    mine = onehot[:, pl.ds(pl.multiple_of(me * TOK, TOK), TOK)]
    slot = lax.broadcasted_iota(jnp.int32, (CLIPS, HEAD_DIM), 0)
    lanes = lax.broadcasted_iota(jnp.int32, (CLIPS, HEAD_DIM), 1)
    partial = jnp.sum(mine * error, axis=1, keepdims=True)
    partial = jnp.sum(jnp.where(slot == lanes, partial, 0.0), axis=0, keepdims=True)
    part_out[...] = partial
    for peer in reversed(peers):
        pltpu.make_async_remote_copy(
            src_ref=part_out,
            dst_ref=part_in.at[me],
            send_sem=part_send.at[0],
            recv_sem=part_recv.at[0],
            device_id=(dp, peer),
            device_id_type=MESH,
        ).start()
    part_in[me] = partial
    wait_for(part_in.at[pl.ds(0, N_SEQ - 1)], part_recv.at[0])
    partial = part_in[0]
    for rank in range(1, N_SEQ):
        partial = partial + part_in[rank]
    losses = partial / size_row
    pl.semaphore_wait(cross_sem, len(across))
    loss_out[...] = losses
    for dx, dy in GROUPS:
        pltpu.make_async_remote_copy(
            src_ref=loss_out,
            dst_ref=loss_in.at[dp],
            send_sem=loss_send.at[0],
            recv_sem=loss_recv.at[0],
            device_id=(lax.rem(dp // 8 + dx, 4) * 8 + lax.rem(dp % 8 + dy, 8), me),
            device_id_type=MESH,
        ).start()
    loss_in[dp] = losses
    wait_for(loss_in.at[pl.ds(0, N_DP - 1)], loss_recv.at[0])
    scores = jnp.zeros((CLIPS, HEAD_DIM), F32)
    for group in range(N_DP):
        scores = scores + jnp.where(wanted == group * CLIPS, loss_in[group], 0.0)
    scores = jnp.sum(scores, axis=1, keepdims=True)
    out_ref[...] = jnp.sum(jnp.where(slot == lanes, scores, 0.0), axis=0, keepdims=True)

    for t in range(3):
        wait_for(qbuf.at[pl.ds(0, (N_SEQ - 1) * TOK)], in_send.at[t])
    wait_for(taken.at[pl.ds(0, 6)], pair_send.at[0])
    wait_for(gathered.at[pl.ds(0, 9)], msg_send.at[0])
    wait_for(part_in.at[pl.ds(0, N_SEQ - 1)], part_send.at[0])
    wait_for(loss_in.at[pl.ds(0, N_DP - 1)], loss_send.at[0])


def per_device(
    queries, keys, values, text_kv, text_lengths, clip_lengths, timesteps, mod_weight, final_weight, noise, clean, report_order
):
    text = text_kv.reshape(CLIPS, 2 * TEXT, HEAD_DIM)
    anywhere = pl.BlockSpec(memory_space=pl.ANY)
    vmem = pl.BlockSpec(memory_space=pltpu.VMEM)
    dma = pltpu.SemaphoreType.DMA
    out = pl.pallas_call(
        kernel,
        out_shape=jax.ShapeDtypeStruct((1, HEAD_DIM), F32),
        in_specs=[anywhere] * 12,
        out_specs=vmem,
        scratch_shapes=[
            pltpu.VMEM((ROWS, HEAD_DIM), BF16),
            pltpu.VMEM((ROWS + 2 * PAD, HEAD_DIM), BF16),
            pltpu.VMEM((ROWS + 2 * PAD, HEAD_DIM), BF16),
            pltpu.VMEM((CLIPS, 2 * TEXT, HEAD_DIM), BF16),
            pltpu.VMEM((FREQ, 2 * WIDTH), BF16),
            pltpu.VMEM((CHANNELS, WIDTH), BF16),
            pltpu.VMEM((CHANNELS, TOK), F32),
            pltpu.VMEM((CHANNELS, TOK), F32),
            pltpu.SMEM((CLIPS,), jnp.int32),
            pltpu.SMEM((1, CLIPS), jnp.int32),
            pltpu.SMEM((CLIPS,), jnp.int32),
            pltpu.SMEM((CLIPS,), jnp.int32),
            pltpu.VMEM((CLIPS * TEXT, HEAD_DIM), BF16),
            pltpu.VMEM((CLIPS * TEXT, HEAD_DIM), BF16),
            pltpu.VMEM((ROWS, HEAD_DIM), BF16),
            pltpu.VMEM((ROWS + 2 * PAD, HEAD_DIM), BF16),
            pltpu.VMEM((CLIPS * TEXT, HEAD_DIM), BF16),
            pltpu.VMEM((CLIPS, ROWS), F32),
            pltpu.VMEM((CLIPS, ROWS), jnp.int32),
            pltpu.VMEM((CLIPS * CHANNELS, 2 * HEAD_DIM), BF16),
            pltpu.VMEM((CHANNELS, TOK), F32),
            pltpu.VMEM((CHANNELS, TOK), F32),
            pltpu.VMEM((CHANNELS, TOK), F32),
            pltpu.VMEM((ROWS, HEAD_DIM), F32),
            pltpu.VMEM((ROWS, HEAD_DIM), F32),
            pltpu.VMEM((ROWS, HEAD_DIM), F32),
            pltpu.VMEM((ROWS, HEAD_DIM), F32),
            pltpu.VMEM((12, 5 * BLOCK, BLOCK), BF16),
            pltpu.VMEM((12 * BLOCK, HEAD_DIM), F32),
            pltpu.VMEM((8, 2, MSG, TOK), BF16),
            pltpu.VMEM((8, MSG, TOK), BF16),
            pltpu.VMEM((8, MSG, TOK), BF16),
            pltpu.VMEM((N_SEQ, MSG, TOK), BF16),
            pltpu.VMEM((1, HEAD_DIM), F32),
            pltpu.VMEM((N_SEQ, 1, HEAD_DIM), F32),
            pltpu.VMEM((1, HEAD_DIM), F32),
            pltpu.VMEM((N_DP, 1, HEAD_DIM), F32),
            pltpu.SemaphoreType.REGULAR,
            pltpu.SemaphoreType.REGULAR,
            dma((9,)),
            dma((3,)),
            dma((2,)),
            dma((8,)),
            dma((1,)),
            dma((8,)),
            dma((1,)),
            dma((1,)),
            dma((1,)),
            dma((1,)),
            dma((1,)),
            dma((1,)),
        ],
        compiler_params=pltpu.CompilerParams(
            collective_id=0, has_side_effects=True, vmem_limit_bytes=60 * 1024 * 1024
        ),
    )(
        queries, keys, values, text, text_lengths, clip_lengths, report_order, timesteps, mod_weight, final_weight.T, noise.T, clean.T
    )
    return out[0, :CLIPS]


def solution(mesh):
    rows = P(("dp", "seq"), None)
    in_specs = (
        rows, rows, rows, P("dp", None, None, "seq"), P("dp"), P("dp", None), P("dp"), P(), P(), rows, rows, P("dp"),
    )
    return jax.shard_map(per_device, mesh=mesh, in_specs=in_specs, out_specs=P("dp"), check_vma=False)
```

```python
import functools
import math

import jax
import jax.numpy as jnp
from jax import lax
from jax.experimental import pallas as pl
from jax.experimental.pallas import tpu as pltpu
from jax.sharding import PartitionSpec as P

MESH = pl.DeviceIdType.MESH
HEAD_DIM = 128
FREQ = 256
CLIPS = 8
TEXT = 256
CHANNELS = 64
WIDTH = 2048
TOK = 128
N_SEQ = 16
N_DP = 32
ROWS = TOK * N_SEQ
BLOCK = 256
BLOCKS = ROWS // BLOCK
PAD = 512
WINDOW = BLOCK + 2 * PAD
NEAR_CLIPS = 5
SPAN = NEAR_CLIPS * TEXT
MSG = 80
FAR = 65536.0
EPS = 1e-06
SCALE = math.log2(math.e) / math.sqrt(HEAD_DIM)
NT = (((1,), (1,)), ((), ()))
F32 = jnp.float32
BF16 = jnp.bfloat16


def nt_dot(a, b):
    return lax.dot_general(a, b, NT, preferred_element_type=F32)


def nn_dot(a, b):
    return jnp.dot(a, b, preferred_element_type=F32)


def pieces(x, count):
    out = []
    for _ in range(count):
        piece = x.astype(BF16)
        out.append(piece)
        x = x - piece.astype(F32)
    return out


def along(scalars, shape, dim):
    place = lax.broadcasted_iota(jnp.int32, shape, dim)
    out = jnp.zeros(shape, jnp.int32)
    for index, scalar in enumerate(scalars):
        out = jnp.where(place == index, scalar, out)
    return out


PARTNERS = [(0, 1), (1, 0), (-1, 0), (1, 1), (-1, 1), (2, 0), (-2, 0), (2, 1), (-2, 1)]
NEAR = len(PARTNERS)
PARTNERS += [(3, 0), (-3, 0), (3, 1), (-3, 1), (4, 0), (4, 1)]


GROUPS = sorted(
    [(dx, dy) for dx in range(4) for dy in range(8) if dx or dy],
    key=lambda step: -(min(step[0], 4 - step[0]) + min(step[1], 8 - step[1])),
)
SOURCES = [0, 4, 3, -3, 2, -2, 1, -1]
EARLY = 6
FINISH = [4, -3, 3, 2, -2, 1, -1, 0]


def wait_for(buffer, sem):
    pltpu.make_async_copy(buffer, buffer, sem).wait()


def kernel(
    q_hbm, k_hbm, v_hbm, text_hbm, tlen_hbm, clen_hbm, order_hbm, time_hbm, modw_hbm, finw_hbm, noise_hbm, clean_hbm,
    out_ref,
    qbuf, kbuf, vbuf, textbuf, modw, finw, noise, clean, tlen_ref, clen_ref, order_ref, time_ref,
    tk, tv, qbias, kbias, tbias, onehot, clip_row, wall, btok, ctok, target,
    text_max, text_sum, text_out, inverse, weights, mixed_out, pair, taken, message, gathered, part_out, part_in, loss_out, loss_in,
    far_sem, cross_sem, load_sem, in_send, in_recv, value_recv, pair_send, pair_recv, msg_send, msg_recv, part_send, part_recv, loss_send, loss_recv,
):
    me = lax.axis_index("seq")
    dp = lax.axis_index("dp")
    z = me // 2
    core = me % 2
    peers = [lax.rem(z + dz + 8, 8) * 2 + lax.rem(core + dc, 2) for dz, dc in PARTNERS]

    barrier = pltpu.get_barrier_semaphore()
    for peer in peers[:NEAR]:
        pl.semaphore_signal(barrier, inc=1, device_id=(dp, peer), device_id_type=MESH)
    others = [lax.rem(dp // 8 + dx, 4) * 8 + lax.rem(lax.rem(dp, 8) + dy, 8) for dx, dy in GROUPS]
    across = [lax.rem(dp // 8 + i, 4) * 8 + lax.rem(dp, 8) for i in range(1, 4)]
    down = [dp // 8 * 8 + lax.rem(lax.rem(dp, 8) + i, 8) for i in range(1, 8)]
    for group in across + down:
        pl.semaphore_signal(barrier, inc=1, device_id=(group, me), device_id_type=MESH)

    streams = [(q_hbm, qbuf, 0), (k_hbm, kbuf, PAD), (v_hbm, vbuf, PAD)]
    pl.semaphore_wait(barrier, NEAR + len(across) + len(down))
    for dz in (2, -2):
        pl.semaphore_signal(far_sem, inc=1, device_id=(dp, lax.rem(z + dz + 8, 8) * 2 + core), device_id_type=MESH)
    for group in across:
        pl.semaphore_signal(cross_sem, inc=1, device_id=(group, me), device_id_type=MESH)

    def send_part(t, partners):
        src, dst, base = streams[t]
        for dz, dc in partners:
            peer = lax.rem(z + dz + 8, 8) * 2 + lax.rem(core + dc, 2)
            pltpu.make_async_remote_copy(
                src_ref=src.at[:, pl.ds(pl.multiple_of(peer * HEAD_DIM, HEAD_DIM), HEAD_DIM)],
                dst_ref=dst.at[pl.ds(pl.multiple_of(base + me * TOK, TOK), TOK)],
                send_sem=in_send.at[t],
                recv_sem=in_recv.at[t] if t < 2 else value_recv.at[dz % 8],
                device_id=(dp, peer),
                device_id_type=MESH,
            ).start()

    send_part(0, PARTNERS[:NEAR][::-1])
    pl.semaphore_wait(far_sem, 2)
    send_part(0, PARTNERS[NEAR:][::-1])
    loads = [
        pltpu.make_async_copy(src, dst, load_sem.at[i])
        for i, (src, dst) in enumerate(
            [
                (tlen_hbm, tlen_ref), (clen_hbm, clen_ref), (order_hbm, order_ref), (time_hbm, time_ref),
                (text_hbm, textbuf), (modw_hbm, modw), (finw_hbm, finw), (noise_hbm, noise), (clean_hbm, clean),
            ]
        )
    ]
    for load in loads:
        load.start()
    head_at = pl.multiple_of(me * HEAD_DIM, HEAD_DIM)
    for t, (src, dst, base) in enumerate(streams):
        pltpu.make_async_copy(
            src.at[:, pl.ds(head_at, HEAD_DIM)],
            dst.at[pl.ds(pl.multiple_of(base + me * TOK, TOK), TOK)],
            in_recv.at[t] if t < 2 else value_recv.at[0],
        ).start()

    send_part(1, PARTNERS[::-1])
    send_part(2, PARTNERS[::-1])
    for load in loads[:4]:
        load.wait()

    starts, ends = [], []
    total = jnp.int32(0)
    for c in range(CLIPS):
        starts.append(total)
        total = total + clen_ref[0, c]
        ends.append(total)
    start_lane, end_lane = along(starts, (1, HEAD_DIM), 1), along(ends, (1, HEAD_DIM), 1)
    start_col, end_col = along(starts, (CLIPS, 1), 0), along(ends, (CLIPS, 1), 0)
    size_row = jnp.where(end_lane > start_lane, end_lane - start_lane, 1).astype(F32)
    place = lax.broadcasted_iota(jnp.int32, (CLIPS, ROWS), 1)
    onehot[...] = jnp.where((place >= start_col) & (place < end_col), 1.0, 0.0)
    clip_of = jnp.zeros((CLIPS, ROWS), jnp.int32)
    for c in range(1, CLIPS):
        clip_of = clip_of + jnp.where(place >= starts[c], 1, 0)
    clip_row[...] = clip_of
    edge = jnp.zeros((PAD, HEAD_DIM), BF16)
    for buf in (kbuf, vbuf):
        buf[pl.ds(0, PAD), :] = edge
        buf[pl.ds(PAD + ROWS, PAD), :] = edge

    rows_iota = lax.broadcasted_iota(jnp.int32, (BLOCK, HEAD_DIM), 0)
    lane_iota = lax.broadcasted_iota(jnp.int32, (BLOCK, HEAD_DIM), 1)

    def fill_key_bias(i, _):
        token = rows_iota + (i * BLOCK - PAD)
        live = (token >= start_lane) & (token < end_lane)
        kbias[pl.ds(pl.multiple_of(i * BLOCK, BLOCK), BLOCK), :] = jnp.where(live, 0.0, -FAR).astype(BF16)
        return 0

    def fill_query_bias(i, _):
        token = rows_iota + i * BLOCK
        live = (token >= start_lane) & (token < end_lane)
        qbias[pl.ds(pl.multiple_of(i * BLOCK, BLOCK), BLOCK), :] = jnp.where(live, 1.0, 0.0).astype(BF16)
        return 0

    lax.fori_loop(0, (ROWS + 2 * PAD) // BLOCK, fill_key_bias, 0)
    lax.fori_loop(0, BLOCKS, fill_query_bias, 0)

    loads[4].wait()
    sub = lax.broadcasted_iota(jnp.int32, (TEXT, 2 * TEXT), 0)
    lane = lax.broadcasted_iota(jnp.int32, (TEXT, 2 * TEXT), 1)
    pick_key = jnp.where(lane == 2 * sub, 1.0, 0.0).astype(BF16)
    pick_value = jnp.where(lane == 2 * sub + 1, 1.0, 0.0).astype(BF16)
    length_lane = along([tlen_ref[c] for c in range(CLIPS)], (1, HEAD_DIM), 1)

    def split_text(c, _):
        both = textbuf[c]
        rows = pl.ds(pl.multiple_of(c * TEXT, TEXT), TEXT)
        tk[rows, :] = nn_dot(pick_key, both).astype(BF16)
        tv[rows, :] = nn_dot(pick_value, both).astype(BF16)
        live = (lane_iota == c) & (rows_iota < length_lane)
        tbias[rows, :] = jnp.where(live, 0.0, -FAR).astype(BF16)
        return 0

    lax.fori_loop(0, CLIPS, split_text, 0)

    loads[5].wait()
    loads[6].wait()
    step = along([time_ref[c] for c in range(CLIPS)], (CLIPS, FREQ // 2), 0).astype(F32)
    ramp = lax.broadcasted_iota(jnp.int32, (CLIPS, FREQ // 2), 1).astype(F32)
    angles = step * jnp.exp(-math.log(10000.0) * ramp / (FREQ // 2))
    embedding = jnp.concatenate([jnp.cos(angles), jnp.sin(angles)], axis=1)
    act = jax.nn.silu(embedding).astype(BF16)
    gain = 1.0 + nn_dot(act, modw[:, pl.ds(WIDTH + head_at, HEAD_DIM)])
    turned = finw[:, pl.ds(head_at, HEAD_DIM)].astype(F32)
    for c in range(CLIPS):
        high, low = pieces(turned * gain[c : c + 1, :], 2)
        wall[pl.ds(c * CHANNELS, CHANNELS), :] = jnp.concatenate([high, low], axis=1)
    shift_all = nn_dot(act, modw[:, pl.ds(0, WIDTH)])
    gain_all = 1.0 + nn_dot(act, modw[:, pl.ds(WIDTH, WIDTH)])
    stacked = jnp.concatenate(pieces(gain_all, 3) + pieces(shift_all, 3), axis=0)
    folded = nt_dot(finw[...], stacked)
    gain_sum = folded[:, 0:8] + folded[:, 8:16] + folded[:, 16:24]
    shift_sum = folded[:, 24:32] + folded[:, 32:40] + folded[:, 40:48]
    mine = onehot[:, pl.ds(pl.multiple_of(me * TOK, TOK), TOK)]
    gain_tok = jnp.zeros((CHANNELS, TOK), F32)
    shift_tok = jnp.zeros((CHANNELS, TOK), F32)
    for c in range(CLIPS):
        gain_tok = gain_tok + gain_sum[:, c : c + 1] * mine[c : c + 1, :]
        shift_tok = shift_tok + shift_sum[:, c : c + 1] * mine[c : c + 1, :]
    btok[...] = gain_tok
    ctok[...] = shift_tok
    loads[7].wait()
    loads[8].wait()
    target[...] = noise[...] - clean[...]
    order_col = along([order_ref[c] for c in range(CLIPS)], (CLIPS, HEAD_DIM), 0)
    order_lane = lax.broadcasted_iota(jnp.int32, (CLIPS, HEAD_DIM), 1)
    wanted = jnp.where(order_lane < CLIPS, order_col - order_lane, -1)

    wait_for(qbuf, in_recv.at[0])
    one_lanes = jnp.ones((SPAN, HEAD_DIM), BF16)

    def text_block(b, _):
        rows = pl.ds(pl.multiple_of(b * BLOCK, BLOCK), BLOCK)
        span = pl.ds(pl.multiple_of(b // 2 * TEXT, TEXT), SPAN)
        left = jnp.concatenate([qbuf[rows, :], qbias[rows, :]], axis=1)
        right = jnp.concatenate([tk[span, :], tbias[span, :]], axis=1)
        scores = nt_dot(left, right)
        top = jnp.max(scores, axis=1, keepdims=True)
        weight = jnp.exp2((scores - top) * SCALE).astype(BF16)
        mixed = nn_dot(weight, jnp.concatenate([tv[span, :], one_lanes], axis=1))
        text_max[rows, :] = jnp.broadcast_to(top, (BLOCK, HEAD_DIM))
        text_out[rows, :] = mixed[:, :HEAD_DIM]
        text_sum[rows, :] = mixed[:, HEAD_DIM:]
        return 0

    lax.fori_loop(0, BLOCKS, text_block, 0)

    wait_for(kbuf.at[pl.ds(PAD, ROWS)], in_recv.at[1])

    def score_block(b, _):
        rows = pl.ds(pl.multiple_of(b * BLOCK, BLOCK), BLOCK)
        window = pl.ds(pl.multiple_of(b * BLOCK, BLOCK), WINDOW)
        left = jnp.concatenate([qbuf[rows, :], qbias[rows, :]], axis=1)
        right = jnp.concatenate([kbuf[window, :], kbias[window, :]], axis=1)
        scores = nt_dot(left, right)
        before = text_max[rows, :]
        top = jnp.maximum(before, jnp.max(scores, axis=1, keepdims=True))
        weight = jnp.exp2((scores - top[:, :1]) * SCALE)
        video_sum = jnp.sum(weight, axis=1, keepdims=True)
        weight = weight.astype(BF16)
        for t in range(5):
            weights[b + t, pl.ds((4 - t) * BLOCK, BLOCK), :] = weight[:, t * BLOCK : (t + 1) * BLOCK]
        fade = jnp.exp2((before - top) * SCALE)
        inv = 1.0 / (video_sum + text_sum[rows, :] * fade)
        inverse[rows, :] = inv
        text_out[rows, :] = text_out[rows, :] * (fade * inv)
        return 0

    lax.fori_loop(0, BLOCKS, score_block, 0, unroll=2)

    mixed_out[...] = jnp.zeros(mixed_out.shape, F32)

    def value_rows(dz):
        chip = lax.rem(z - dz + 8, 8)
        wait_for(vbuf.at[pl.ds(PAD, BLOCK)], value_recv.at[dz % 8])
        return chip, vbuf[pl.ds(pl.multiple_of(PAD + chip * BLOCK, BLOCK), BLOCK), :]

    def add_source(dz):
        chip, rows = value_rows(dz)
        around = pl.ds(pl.multiple_of(chip * BLOCK, BLOCK), 5 * BLOCK)
        mixed_out[around, :] = mixed_out[around, :] + nn_dot(weights[chip + 2], rows)

    ones_rows = jnp.ones((16, HEAD_DIM), BF16)
    zero_rows = jnp.zeros((16, HEAD_DIM), BF16)
    count_left = jnp.concatenate([ones_rows, zero_rows], axis=1)
    count_both = jnp.concatenate([ones_rows, ones_rows], axis=1)
    row16 = lax.broadcasted_iota(jnp.int32, (16, TOK), 0)
    wide16 = lax.broadcasted_iota(jnp.int32, (16, BLOCK), 0)

    def stat_rows(place, total, squares):
        total_high, total_low = [x.astype(F32) for x in pieces(total, 2)]
        square_high, square_low = [x.astype(F32) for x in pieces(squares, 2)]
        rows = jnp.where(place == 2, square_high, jnp.where(place == 3, square_low, 0.0))
        return jnp.where(place == 0, total_high, jnp.where(place == 1, total_low, rows))

    def project(b):
        rows = pl.ds(pl.multiple_of(b * BLOCK, BLOCK), BLOCK)
        first = b // 2
        mixed = mixed_out[pl.ds(pl.multiple_of((b + 2) * BLOCK, BLOCK), BLOCK), :]
        attended = (mixed * inverse[rows, :] + text_out[rows, :]).astype(BF16)
        fold = wall[pl.ds(pl.multiple_of(first * CHANNELS, CHANNELS), NEAR_CLIPS * CHANNELS), :]
        spread = nt_dot(jnp.concatenate([fold, count_left], axis=0), jnp.concatenate([attended, attended], axis=1))
        clip_here = clip_row[0:1, rows]
        picked = spread[:CHANNELS]
        for j in range(1, NEAR_CLIPS):
            picked = jnp.where(clip_here == first + j, spread[j * CHANNELS : (j + 1) * CHANNELS], picked)
        wide = attended.astype(F32)
        squares = nt_dot(count_both, jnp.concatenate(pieces(wide * wide, 2), axis=1))
        stats = stat_rows(wide16, spread[NEAR_CLIPS * CHANNELS :], squares)
        full = jnp.concatenate([picked, stats], axis=0).astype(BF16)
        pair[b, 0] = full[:, :TOK]
        pair[b, 1] = full[:, TOK:]

    def exchange(i, b):
        copy = pltpu.make_async_remote_copy(
            src_ref=pair.at[b, 1 - core],
            dst_ref=taken.at[b],
            send_sem=pair_send.at[0],
            recv_sem=pair_recv.at[i],
            device_id=(dp, z * 2 + 1 - core),
            device_id_type=MESH,
        )
        copy.start()
        return copy

    def message_copy(source, slot, owner):
        pltpu.make_async_remote_copy(
            src_ref=source,
            dst_ref=gathered.at[slot],
            send_sem=msg_send.at[0],
            recv_sem=msg_recv.at[0],
            device_id=(dp, owner),
            device_id_type=MESH,
        ).start()

    def deliver(i, b, copy):
        copy.wait_recv()
        both = pair[b, core].astype(F32) + taken[b].astype(F32)
        stats = stat_rows(row16, both[64:65] + both[65:66], both[66:67] + both[67:68])
        total = jnp.concatenate([both[:CHANNELS], stats], axis=0).astype(BF16)
        if FINISH[i] == 0:
            gathered[2 * z] = total
            return
        message[b] = total
        message_copy(message.at[b], 2 * z, b * 2 + core)

    def finish(i):
        b = lax.rem(z + FINISH[i] + 8, 8)
        project(b)
        if abs(FINISH[i]) == 9:
            for to in range(2):
                message_copy(pair.at[b, to], me, b * 2 + to)
            return None
        return i, b, exchange(i, b)

    for dz in SOURCES[:EARLY]:
        add_source(dz)
    waiting = [finish(0)]
    add_source(SOURCES[EARLY])
    waiting.append(finish(1))
    add_source(SOURCES[EARLY + 1])
    for i in range(2, len(FINISH)):
        waiting.append(finish(i))
    for entry in waiting:
        if entry is not None:
            deliver(*entry)

    wait_for(gathered.at[pl.ds(0, 7)], msg_recv.at[0])
    total = gathered[2 * z].astype(F32)
    for dz in (1, 2, 3, 4, 5, 6, 7):
        chip = lax.rem(z + dz, 8)
        total = total + gathered[2 * chip].astype(F32)
        if dz in ():
            total = total + gathered[2 * chip + 1].astype(F32)
    center = (total[64:65] + total[65:66]) / WIDTH
    spread = (total[66:67] + total[67:68]) / WIDTH - center * center
    predicted = lax.rsqrt(spread + EPS) * (total[:CHANNELS] - center * btok[...]) + ctok[...]
    difference = predicted - target[...]
    error = jnp.sum(difference * difference, axis=0, keepdims=True) / CHANNELS
    mine = onehot[:, pl.ds(pl.multiple_of(me * TOK, TOK), TOK)]
    slot = lax.broadcasted_iota(jnp.int32, (CLIPS, HEAD_DIM), 0)
    lanes = lax.broadcasted_iota(jnp.int32, (CLIPS, HEAD_DIM), 1)
    partial = jnp.sum(mine * error, axis=1, keepdims=True)
    partial = jnp.sum(jnp.where(slot == lanes, partial, 0.0), axis=0, keepdims=True)
    part_out[...] = partial
    for peer in reversed(peers):
        pltpu.make_async_remote_copy(
            src_ref=part_out,
            dst_ref=part_in.at[me],
            send_sem=part_send.at[0],
            recv_sem=part_recv.at[0],
            device_id=(dp, peer),
            device_id_type=MESH,
        ).start()
    part_in[me] = partial
    wait_for(part_in.at[pl.ds(0, N_SEQ - 1)], part_recv.at[0])
    partial = part_in[0]
    for rank in range(1, N_SEQ):
        partial = partial + part_in[rank]
    losses = partial / size_row
    pl.semaphore_wait(cross_sem, len(across))
    loss_out[...] = losses
    for group in others:
        pltpu.make_async_remote_copy(
            src_ref=loss_out,
            dst_ref=loss_in.at[dp],
            send_sem=loss_send.at[0],
            recv_sem=loss_recv.at[0],
            device_id=(group, me),
            device_id_type=MESH,
        ).start()
    loss_in[dp] = losses
    wait_for(loss_in.at[pl.ds(0, N_DP - 1)], loss_recv.at[0])
    scores = jnp.zeros((CLIPS, HEAD_DIM), F32)
    for group in range(N_DP):
        scores = scores + jnp.where(wanted == group * CLIPS, loss_in[group], 0.0)
    scores = jnp.sum(scores, axis=1, keepdims=True)
    out_ref[...] = jnp.sum(jnp.where(slot == lanes, scores, 0.0), axis=0, keepdims=True)

    for t in range(3):
        wait_for(qbuf.at[pl.ds(0, (N_SEQ - 1) * TOK)], in_send.at[t])
    wait_for(taken.at[pl.ds(0, 8)], pair_send.at[0])
    wait_for(gathered.at[pl.ds(0, 7)], msg_send.at[0])
    wait_for(part_in.at[pl.ds(0, N_SEQ - 1)], part_send.at[0])
    wait_for(loss_in.at[pl.ds(0, N_DP - 1)], loss_send.at[0])


def per_device(
    queries, keys, values, text_kv, text_lengths, clip_lengths, timesteps, mod_weight, final_weight, noise, clean, report_order
):
    text = text_kv.reshape(CLIPS, 2 * TEXT, HEAD_DIM)
    anywhere = pl.BlockSpec(memory_space=pl.ANY)
    vmem = pl.BlockSpec(memory_space=pltpu.VMEM)
    dma = pltpu.SemaphoreType.DMA
    out = pl.pallas_call(
        kernel,
        out_shape=jax.ShapeDtypeStruct((1, HEAD_DIM), F32),
        in_specs=[anywhere] * 12,
        out_specs=vmem,
        scratch_shapes=[
            pltpu.VMEM((ROWS, HEAD_DIM), BF16),
            pltpu.VMEM((ROWS + 2 * PAD, HEAD_DIM), BF16),
            pltpu.VMEM((ROWS + 2 * PAD, HEAD_DIM), BF16),
            pltpu.VMEM((CLIPS, 2 * TEXT, HEAD_DIM), BF16),
            pltpu.VMEM((FREQ, 2 * WIDTH), BF16),
            pltpu.VMEM((CHANNELS, WIDTH), BF16),
            pltpu.VMEM((CHANNELS, TOK), F32),
            pltpu.VMEM((CHANNELS, TOK), F32),
            pltpu.SMEM((CLIPS,), jnp.int32),
            pltpu.SMEM((1, CLIPS), jnp.int32),
            pltpu.SMEM((CLIPS,), jnp.int32),
            pltpu.SMEM((CLIPS,), jnp.int32),
            pltpu.VMEM((CLIPS * TEXT, HEAD_DIM), BF16),
            pltpu.VMEM((CLIPS * TEXT, HEAD_DIM), BF16),
            pltpu.VMEM((ROWS, HEAD_DIM), BF16),
            pltpu.VMEM((ROWS + 2 * PAD, HEAD_DIM), BF16),
            pltpu.VMEM((CLIPS * TEXT, HEAD_DIM), BF16),
            pltpu.VMEM((CLIPS, ROWS), F32),
            pltpu.VMEM((CLIPS, ROWS), jnp.int32),
            pltpu.VMEM((CLIPS * CHANNELS, 2 * HEAD_DIM), BF16),
            pltpu.VMEM((CHANNELS, TOK), F32),
            pltpu.VMEM((CHANNELS, TOK), F32),
            pltpu.VMEM((CHANNELS, TOK), F32),
            pltpu.VMEM((ROWS, HEAD_DIM), F32),
            pltpu.VMEM((ROWS, HEAD_DIM), F32),
            pltpu.VMEM((ROWS, HEAD_DIM), F32),
            pltpu.VMEM((ROWS, HEAD_DIM), F32),
            pltpu.VMEM((12, 5 * BLOCK, BLOCK), BF16),
            pltpu.VMEM((12 * BLOCK, HEAD_DIM), F32),
            pltpu.VMEM((8, 2, MSG, TOK), BF16),
            pltpu.VMEM((8, MSG, TOK), BF16),
            pltpu.VMEM((8, MSG, TOK), BF16),
            pltpu.VMEM((N_SEQ, MSG, TOK), BF16),
            pltpu.VMEM((1, HEAD_DIM), F32),
            pltpu.VMEM((N_SEQ, 1, HEAD_DIM), F32),
            pltpu.VMEM((1, HEAD_DIM), F32),
            pltpu.VMEM((N_DP, 1, HEAD_DIM), F32),
            pltpu.SemaphoreType.REGULAR,
            pltpu.SemaphoreType.REGULAR,
            dma((9,)),
            dma((3,)),
            dma((2,)),
            dma((8,)),
            dma((1,)),
            dma((8,)),
            dma((1,)),
            dma((1,)),
            dma((1,)),
            dma((1,)),
            dma((1,)),
            dma((1,)),
        ],
        compiler_params=pltpu.CompilerParams(
            collective_id=0, has_side_effects=True, vmem_limit_bytes=40 * 1024 * 1024
        ),
    )(*[pltpu.with_memory_space_constraint(operand, pltpu.HBM) for operand in (
        queries, keys, values, text, text_lengths, clip_lengths, report_order, timesteps, mod_weight, final_weight.T, noise.T, clean.T
    )])
    return out[0, :CLIPS]


def solution(mesh):
    rows = P(("dp", "seq"), None)
    in_specs = (
        rows, rows, rows, P("dp", None, None, "seq"), P("dp"), P("dp", None), P("dp"), P(), P(), rows, rows, P("dp"),
    )
    return jax.shard_map(per_device, mesh=mesh, in_specs=in_specs, out_specs=P("dp"), check_vma=False)
```

```python
import functools
import math

import jax
import jax.numpy as jnp
from jax import lax
from jax.experimental import pallas as pl
from jax.experimental.pallas import tpu as pltpu
from jax.sharding import PartitionSpec as P

MESH = pl.DeviceIdType.MESH
HEAD_DIM = 128
FREQ = 256
CLIPS = 8
TEXT = 256
CHANNELS = 64
WIDTH = 2048
TOK = 128
N_SEQ = 16
N_DP = 32
ROWS = TOK * N_SEQ
BLOCK = 256
BLOCKS = ROWS // BLOCK
PAD = 512
WINDOW = BLOCK + 2 * PAD
NEAR_CLIPS = 5
SPAN = NEAR_CLIPS * TEXT
MSG = 80
FAR = 65536.0
EPS = 1e-06
SCALE = math.log2(math.e) / math.sqrt(HEAD_DIM)
NT = (((1,), (1,)), ((), ()))
F32 = jnp.float32
BF16 = jnp.bfloat16


def nt_dot(a, b):
    return lax.dot_general(a, b, NT, preferred_element_type=F32)


def nn_dot(a, b):
    return jnp.dot(a, b, preferred_element_type=F32)


def pieces(x, count):
    out = []
    for _ in range(count):
        piece = x.astype(BF16)
        out.append(piece)
        x = x - piece.astype(F32)
    return out


def along(scalars, shape, dim):
    place = lax.broadcasted_iota(jnp.int32, shape, dim)
    out = jnp.zeros(shape, jnp.int32)
    for index, scalar in enumerate(scalars):
        out = jnp.where(place == index, scalar, out)
    return out


PARTNERS = [(0, 1), (1, 0), (-1, 0), (1, 1), (-1, 1), (2, 0), (-2, 0), (2, 1), (-2, 1)]
NEAR = len(PARTNERS)
PARTNERS += [(3, 0), (-3, 0), (3, 1), (-3, 1), (4, 0), (4, 1)]


GROUPS = sorted(
    [(dx, dy) for dx in range(4) for dy in range(8) if dx or dy],
    key=lambda step: -(min(step[0], 4 - step[0]) + min(step[1], 8 - step[1])),
)
SOURCES = [0, 4, 3, -3, 2, -2, 1, -1]
EARLY = 6
FINISH = [4, -3, 3, 2, -2, 1, -1, 0]


def wait_for(buffer, sem):
    pltpu.make_async_copy(buffer, buffer, sem).wait()


def kernel(
    q_hbm, k_hbm, v_hbm, text_hbm, tlen_hbm, clen_hbm, order_hbm, time_hbm, modw_hbm, finw_hbm, noise_hbm, clean_hbm,
    out_ref,
    qbuf, kbuf, vbuf, textbuf, modw, finw, noise, clean, tlen_ref, clen_ref, order_ref, time_ref,
    tk, tv, qbias, kbias, tbias, onehot, clip_row, wall, btok, ctok, target,
    text_max, text_sum, text_out, inverse, weights, mixed_out, pair, taken, message, gathered, part_out, part_in, loss_out, loss_in,
    far_sem, cross_sem, load_sem, in_send, in_recv, value_recv, pair_send, pair_recv, msg_send, msg_recv, part_send, part_recv, loss_send, loss_recv,
):
    me = lax.axis_index("seq")
    dp = lax.axis_index("dp")
    z = me // 2
    core = me % 2
    peers = [lax.rem(z + dz + 8, 8) * 2 + lax.rem(core + dc, 2) for dz, dc in PARTNERS]

    barrier = pltpu.get_barrier_semaphore()
    for peer in peers[:NEAR]:
        pl.semaphore_signal(barrier, inc=1, device_id=(dp, peer), device_id_type=MESH)
    others = [lax.rem(dp // 8 + dx, 4) * 8 + lax.rem(lax.rem(dp, 8) + dy, 8) for dx, dy in GROUPS]
    across = [lax.rem(dp // 8 + i, 4) * 8 + lax.rem(dp, 8) for i in range(1, 4)]
    down = [dp // 8 * 8 + lax.rem(lax.rem(dp, 8) + i, 8) for i in range(1, 8)]
    for group in across + down:
        pl.semaphore_signal(barrier, inc=1, device_id=(group, me), device_id_type=MESH)

    streams = [(q_hbm, qbuf, 0), (k_hbm, kbuf, PAD), (v_hbm, vbuf, PAD)]
    pl.semaphore_wait(barrier, NEAR + len(across) + len(down))
    for dz in (2, -2):
        pl.semaphore_signal(far_sem, inc=1, device_id=(dp, lax.rem(z + dz + 8, 8) * 2 + core), device_id_type=MESH)
    for group in across:
        pl.semaphore_signal(cross_sem, inc=1, device_id=(group, me), device_id_type=MESH)

    def send_part(t, partners):
        src, dst, base = streams[t]
        for dz, dc in partners:
            peer = lax.rem(z + dz + 8, 8) * 2 + lax.rem(core + dc, 2)
            pltpu.make_async_remote_copy(
                src_ref=src.at[:, pl.ds(pl.multiple_of(peer * HEAD_DIM, HEAD_DIM), HEAD_DIM)],
                dst_ref=dst.at[pl.ds(pl.multiple_of(base + me * TOK, TOK), TOK)],
                send_sem=in_send.at[t],
                recv_sem=in_recv.at[t] if t < 2 else value_recv.at[dz % 8],
                device_id=(dp, peer),
                device_id_type=MESH,
            ).start()

    send_part(0, PARTNERS[:NEAR][::-1])
    pl.semaphore_wait(far_sem, 2)
    send_part(0, PARTNERS[NEAR:][::-1])
    loads = [
        pltpu.make_async_copy(src, dst, load_sem.at[i])
        for i, (src, dst) in enumerate(
            [
                (tlen_hbm, tlen_ref), (clen_hbm, clen_ref), (order_hbm, order_ref), (time_hbm, time_ref),
                (text_hbm, textbuf), (modw_hbm, modw), (finw_hbm, finw), (noise_hbm, noise), (clean_hbm, clean),
            ]
        )
    ]
    for load in loads:
        load.start()
    head_at = pl.multiple_of(me * HEAD_DIM, HEAD_DIM)
    for t, (src, dst, base) in enumerate(streams):
        pltpu.make_async_copy(
            src.at[:, pl.ds(head_at, HEAD_DIM)],
            dst.at[pl.ds(pl.multiple_of(base + me * TOK, TOK), TOK)],
            in_recv.at[t] if t < 2 else value_recv.at[0],
        ).start()

    send_part(1, PARTNERS[::-1])
    send_part(2, PARTNERS[::-1])
    for load in loads[:4]:
        load.wait()

    starts, ends = [], []
    total = jnp.int32(0)
    for c in range(CLIPS):
        starts.append(total)
        total = total + clen_ref[0, c]
        ends.append(total)
    start_lane, end_lane = along(starts, (1, HEAD_DIM), 1), along(ends, (1, HEAD_DIM), 1)
    start_col, end_col = along(starts, (CLIPS, 1), 0), along(ends, (CLIPS, 1), 0)
    size_row = jnp.where(end_lane > start_lane, end_lane - start_lane, 1).astype(F32)
    place = lax.broadcasted_iota(jnp.int32, (CLIPS, ROWS), 1)
    onehot[...] = jnp.where((place >= start_col) & (place < end_col), 1.0, 0.0)
    clip_of = jnp.zeros((CLIPS, ROWS), jnp.int32)
    for c in range(1, CLIPS):
        clip_of = clip_of + jnp.where(place >= starts[c], 1, 0)
    clip_row[...] = clip_of
    edge = jnp.zeros((PAD, HEAD_DIM), BF16)
    for buf in (kbuf, vbuf):
        buf[pl.ds(0, PAD), :] = edge
        buf[pl.ds(PAD + ROWS, PAD), :] = edge

    rows_iota = lax.broadcasted_iota(jnp.int32, (BLOCK, HEAD_DIM), 0)
    lane_iota = lax.broadcasted_iota(jnp.int32, (BLOCK, HEAD_DIM), 1)

    def fill_key_bias(i, _):
        token = rows_iota + (i * BLOCK - PAD)
        live = (token >= start_lane) & (token < end_lane)
        kbias[pl.ds(pl.multiple_of(i * BLOCK, BLOCK), BLOCK), :] = jnp.where(live, 0.0, -FAR).astype(BF16)
        return 0

    def fill_query_bias(i, _):
        token = rows_iota + i * BLOCK
        live = (token >= start_lane) & (token < end_lane)
        qbias[pl.ds(pl.multiple_of(i * BLOCK, BLOCK), BLOCK), :] = jnp.where(live, 1.0, 0.0).astype(BF16)
        return 0

    lax.fori_loop(0, (ROWS + 2 * PAD) // BLOCK, fill_key_bias, 0)
    lax.fori_loop(0, BLOCKS, fill_query_bias, 0)

    loads[4].wait()
    sub = lax.broadcasted_iota(jnp.int32, (TEXT, 2 * TEXT), 0)
    lane = lax.broadcasted_iota(jnp.int32, (TEXT, 2 * TEXT), 1)
    pick_key = jnp.where(lane == 2 * sub, 1.0, 0.0).astype(BF16)
    pick_value = jnp.where(lane == 2 * sub + 1, 1.0, 0.0).astype(BF16)
    length_lane = along([tlen_ref[c] for c in range(CLIPS)], (1, HEAD_DIM), 1)

    def split_text(c, _):
        both = textbuf[c]
        rows = pl.ds(pl.multiple_of(c * TEXT, TEXT), TEXT)
        tk[rows, :] = nn_dot(pick_key, both).astype(BF16)
        tv[rows, :] = nn_dot(pick_value, both).astype(BF16)
        live = (lane_iota == c) & (rows_iota < length_lane)
        tbias[rows, :] = jnp.where(live, 0.0, -FAR).astype(BF16)
        return 0

    lax.fori_loop(0, CLIPS, split_text, 0)

    loads[5].wait()
    loads[6].wait()
    step = along([time_ref[c] for c in range(CLIPS)], (CLIPS, FREQ // 2), 0).astype(F32)
    ramp = lax.broadcasted_iota(jnp.int32, (CLIPS, FREQ // 2), 1).astype(F32)
    angles = step * jnp.exp(-math.log(10000.0) * ramp / (FREQ // 2))
    embedding = jnp.concatenate([jnp.cos(angles), jnp.sin(angles)], axis=1)
    act = jax.nn.silu(embedding).astype(BF16)
    gain = 1.0 + nn_dot(act, modw[:, pl.ds(WIDTH + head_at, HEAD_DIM)])
    turned = finw[:, pl.ds(head_at, HEAD_DIM)].astype(F32)
    for c in range(CLIPS):
        high, low = pieces(turned * gain[c : c + 1, :], 2)
        wall[pl.ds(c * CHANNELS, CHANNELS), :] = jnp.concatenate([high, low], axis=1)
    shift_all = nn_dot(act, modw[:, pl.ds(0, WIDTH)])
    gain_all = 1.0 + nn_dot(act, modw[:, pl.ds(WIDTH, WIDTH)])
    stacked = jnp.concatenate(pieces(gain_all, 3) + pieces(shift_all, 3), axis=0)
    folded = nt_dot(finw[...], stacked)
    gain_sum = folded[:, 0:8] + folded[:, 8:16] + folded[:, 16:24]
    shift_sum = folded[:, 24:32] + folded[:, 32:40] + folded[:, 40:48]
    mine = onehot[:, pl.ds(pl.multiple_of(me * TOK, TOK), TOK)]
    gain_tok = jnp.zeros((CHANNELS, TOK), F32)
    shift_tok = jnp.zeros((CHANNELS, TOK), F32)
    for c in range(CLIPS):
        gain_tok = gain_tok + gain_sum[:, c : c + 1] * mine[c : c + 1, :]
        shift_tok = shift_tok + shift_sum[:, c : c + 1] * mine[c : c + 1, :]
    btok[...] = gain_tok
    ctok[...] = shift_tok
    loads[7].wait()
    loads[8].wait()
    target[...] = noise[...] - clean[...]
    order_col = along([order_ref[c] for c in range(CLIPS)], (CLIPS, HEAD_DIM), 0)
    order_lane = lax.broadcasted_iota(jnp.int32, (CLIPS, HEAD_DIM), 1)
    wanted = jnp.where(order_lane < CLIPS, order_col - order_lane, -1)

    wait_for(qbuf, in_recv.at[0])
    one_lanes = jnp.ones((SPAN, HEAD_DIM), BF16)

    def text_block(b, _):
        rows = pl.ds(pl.multiple_of(b * BLOCK, BLOCK), BLOCK)
        span = pl.ds(pl.multiple_of(b // 2 * TEXT, TEXT), SPAN)
        left = jnp.concatenate([qbuf[rows, :], qbias[rows, :]], axis=1)
        right = jnp.concatenate([tk[span, :], tbias[span, :]], axis=1)
        scores = nt_dot(left, right)
        top = jnp.max(scores, axis=1, keepdims=True)
        weight = jnp.exp2((scores - top) * SCALE).astype(BF16)
        mixed = nn_dot(weight, jnp.concatenate([tv[span, :], one_lanes], axis=1))
        text_max[rows, :] = jnp.broadcast_to(top, (BLOCK, HEAD_DIM))
        text_out[rows, :] = mixed[:, :HEAD_DIM]
        text_sum[rows, :] = mixed[:, HEAD_DIM:]
        return 0

    lax.fori_loop(0, BLOCKS, text_block, 0)

    wait_for(kbuf.at[pl.ds(PAD, ROWS)], in_recv.at[1])

    def score_block(b, _):
        rows = pl.ds(pl.multiple_of(b * BLOCK, BLOCK), BLOCK)
        window = pl.ds(pl.multiple_of(b * BLOCK, BLOCK), WINDOW)
        left = jnp.concatenate([qbuf[rows, :], qbias[rows, :]], axis=1)
        right = jnp.concatenate([kbuf[window, :], kbias[window, :]], axis=1)
        scores = nt_dot(left, right)
        before = text_max[rows, :]
        top = jnp.maximum(before, jnp.max(scores, axis=1, keepdims=True))
        weight = jnp.exp2((scores - top[:, :1]) * SCALE)
        video_sum = jnp.sum(weight, axis=1, keepdims=True)
        weight = weight.astype(BF16)
        for t in range(5):
            weights[b + t, pl.ds((4 - t) * BLOCK, BLOCK), :] = weight[:, t * BLOCK : (t + 1) * BLOCK]
        fade = jnp.exp2((before - top) * SCALE)
        inv = 1.0 / (video_sum + text_sum[rows, :] * fade)
        inverse[rows, :] = inv
        text_out[rows, :] = text_out[rows, :] * (fade * inv)
        return 0

    lax.fori_loop(0, BLOCKS, score_block, 0, unroll=2)

    mixed_out[...] = jnp.zeros(mixed_out.shape, F32)

    def value_rows(dz):
        chip = lax.rem(z - dz + 8, 8)
        wait_for(vbuf.at[pl.ds(PAD, BLOCK)], value_recv.at[dz % 8])
        return chip, vbuf[pl.ds(pl.multiple_of(PAD + chip * BLOCK, BLOCK), BLOCK), :]

    def add_source(dz):
        chip, rows = value_rows(dz)
        around = pl.ds(pl.multiple_of(chip * BLOCK, BLOCK), 5 * BLOCK)
        mixed_out[around, :] = mixed_out[around, :] + nn_dot(weights[chip + 2], rows)

    ones_rows = jnp.ones((16, HEAD_DIM), BF16)
    zero_rows = jnp.zeros((16, HEAD_DIM), BF16)
    count_left = jnp.concatenate([ones_rows, zero_rows], axis=1)
    count_both = jnp.concatenate([ones_rows, ones_rows], axis=1)
    row16 = lax.broadcasted_iota(jnp.int32, (16, TOK), 0)
    wide16 = lax.broadcasted_iota(jnp.int32, (16, BLOCK), 0)

    def stat_rows(place, total, squares):
        total_high, total_low = [x.astype(F32) for x in pieces(total, 2)]
        square_high, square_low = [x.astype(F32) for x in pieces(squares, 2)]
        rows = jnp.where(place == 2, square_high, jnp.where(place == 3, square_low, 0.0))
        return jnp.where(place == 0, total_high, jnp.where(place == 1, total_low, rows))

    def project(b):
        rows = pl.ds(pl.multiple_of(b * BLOCK, BLOCK), BLOCK)
        first = b // 2
        mixed = mixed_out[pl.ds(pl.multiple_of((b + 2) * BLOCK, BLOCK), BLOCK), :]
        attended = (mixed * inverse[rows, :] + text_out[rows, :]).astype(BF16)
        fold = wall[pl.ds(pl.multiple_of(first * CHANNELS, CHANNELS), NEAR_CLIPS * CHANNELS), :]
        spread = nt_dot(jnp.concatenate([fold, count_left], axis=0), jnp.concatenate([attended, attended], axis=1))
        clip_here = clip_row[0:1, rows]
        picked = spread[:CHANNELS]
        for j in range(1, NEAR_CLIPS):
            picked = jnp.where(clip_here == first + j, spread[j * CHANNELS : (j + 1) * CHANNELS], picked)
        wide = attended.astype(F32)
        squares = nt_dot(count_both, jnp.concatenate(pieces(wide * wide, 2), axis=1))
        stats = stat_rows(wide16, spread[NEAR_CLIPS * CHANNELS :], squares)
        full = jnp.concatenate([picked, stats], axis=0).astype(BF16)
        pair[b, 0] = full[:, :TOK]
        pair[b, 1] = full[:, TOK:]

    def exchange(i, b):
        copy = pltpu.make_async_remote_copy(
            src_ref=pair.at[b, 1 - core],
            dst_ref=taken.at[b],
            send_sem=pair_send.at[0],
            recv_sem=pair_recv.at[i],
            device_id=(dp, z * 2 + 1 - core),
            device_id_type=MESH,
        )
        copy.start()
        return copy

    def message_copy(source, slot, owner):
        pltpu.make_async_remote_copy(
            src_ref=source,
            dst_ref=gathered.at[slot],
            send_sem=msg_send.at[0],
            recv_sem=msg_recv.at[0],
            device_id=(dp, owner),
            device_id_type=MESH,
        ).start()

    def deliver(i, b, copy):
        copy.wait_recv()
        both = pair[b, core].astype(F32) + taken[b].astype(F32)
        stats = stat_rows(row16, both[64:65] + both[65:66], both[66:67] + both[67:68])
        total = jnp.concatenate([both[:CHANNELS], stats], axis=0).astype(BF16)
        if FINISH[i] == 0:
            gathered[2 * z] = total
            return
        message[b] = total
        message_copy(message.at[b], 2 * z, b * 2 + core)

    def finish(i):
        b = lax.rem(z + FINISH[i] + 8, 8)
        project(b)
        if abs(FINISH[i]) == 9:
            for to in range(2):
                message_copy(pair.at[b, to], me, b * 2 + to)
            return None
        return i, b, exchange(i, b)

    for dz in SOURCES[:EARLY]:
        add_source(dz)
    waiting = [finish(0)]
    add_source(SOURCES[EARLY])
    waiting.append(finish(1))
    deliver(*waiting[0])
    add_source(SOURCES[EARLY + 1])
    for i in range(2, len(FINISH)):
        waiting.append(finish(i))
    for entry in waiting[1:]:
        deliver(*entry)

    wait_for(gathered.at[pl.ds(0, 7)], msg_recv.at[0])
    total = gathered[2 * z].astype(F32)
    for dz in (1, 2, 3, 4, 5, 6, 7):
        chip = lax.rem(z + dz, 8)
        total = total + gathered[2 * chip].astype(F32)
        if dz in ():
            total = total + gathered[2 * chip + 1].astype(F32)
    center = (total[64:65] + total[65:66]) / WIDTH
    spread = (total[66:67] + total[67:68]) / WIDTH - center * center
    predicted = lax.rsqrt(spread + EPS) * (total[:CHANNELS] - center * btok[...]) + ctok[...]
    difference = predicted - target[...]
    error = jnp.sum(difference * difference, axis=0, keepdims=True) / CHANNELS
    mine = onehot[:, pl.ds(pl.multiple_of(me * TOK, TOK), TOK)]
    slot = lax.broadcasted_iota(jnp.int32, (CLIPS, HEAD_DIM), 0)
    lanes = lax.broadcasted_iota(jnp.int32, (CLIPS, HEAD_DIM), 1)
    partial = jnp.sum(mine * error, axis=1, keepdims=True)
    partial = jnp.sum(jnp.where(slot == lanes, partial, 0.0), axis=0, keepdims=True)
    part_out[...] = partial
    for peer in reversed(peers):
        pltpu.make_async_remote_copy(
            src_ref=part_out,
            dst_ref=part_in.at[me],
            send_sem=part_send.at[0],
            recv_sem=part_recv.at[0],
            device_id=(dp, peer),
            device_id_type=MESH,
        ).start()
    part_in[me] = partial
    wait_for(part_in.at[pl.ds(0, N_SEQ - 1)], part_recv.at[0])
    partial = part_in[0]
    for rank in range(1, N_SEQ):
        partial = partial + part_in[rank]
    losses = partial / size_row
    pl.semaphore_wait(cross_sem, len(across))
    loss_out[...] = losses
    for group in others:
        pltpu.make_async_remote_copy(
            src_ref=loss_out,
            dst_ref=loss_in.at[dp],
            send_sem=loss_send.at[0],
            recv_sem=loss_recv.at[0],
            device_id=(group, me),
            device_id_type=MESH,
        ).start()
    loss_in[dp] = losses
    wait_for(loss_in.at[pl.ds(0, N_DP - 1)], loss_recv.at[0])
    scores = jnp.zeros((CLIPS, HEAD_DIM), F32)
    for group in range(N_DP):
        scores = scores + jnp.where(wanted == group * CLIPS, loss_in[group], 0.0)
    scores = jnp.sum(scores, axis=1, keepdims=True)
    out_ref[...] = jnp.sum(jnp.where(slot == lanes, scores, 0.0), axis=0, keepdims=True)

    for t in range(3):
        wait_for(qbuf.at[pl.ds(0, (N_SEQ - 1) * TOK)], in_send.at[t])
    wait_for(taken.at[pl.ds(0, 8)], pair_send.at[0])
    wait_for(gathered.at[pl.ds(0, 7)], msg_send.at[0])
    wait_for(part_in.at[pl.ds(0, N_SEQ - 1)], part_send.at[0])
    wait_for(loss_in.at[pl.ds(0, N_DP - 1)], loss_send.at[0])


def per_device(
    queries, keys, values, text_kv, text_lengths, clip_lengths, timesteps, mod_weight, final_weight, noise, clean, report_order
):
    text = text_kv.reshape(CLIPS, 2 * TEXT, HEAD_DIM)
    anywhere = pl.BlockSpec(memory_space=pl.ANY)
    vmem = pl.BlockSpec(memory_space=pltpu.VMEM)
    dma = pltpu.SemaphoreType.DMA
    out = pl.pallas_call(
        kernel,
        out_shape=jax.ShapeDtypeStruct((1, HEAD_DIM), F32),
        in_specs=[anywhere] * 12,
        out_specs=vmem,
        scratch_shapes=[
            pltpu.VMEM((ROWS, HEAD_DIM), BF16),
            pltpu.VMEM((ROWS + 2 * PAD, HEAD_DIM), BF16),
            pltpu.VMEM((ROWS + 2 * PAD, HEAD_DIM), BF16),
            pltpu.VMEM((CLIPS, 2 * TEXT, HEAD_DIM), BF16),
            pltpu.VMEM((FREQ, 2 * WIDTH), BF16),
            pltpu.VMEM((CHANNELS, WIDTH), BF16),
            pltpu.VMEM((CHANNELS, TOK), F32),
            pltpu.VMEM((CHANNELS, TOK), F32),
            pltpu.SMEM((CLIPS,), jnp.int32),
            pltpu.SMEM((1, CLIPS), jnp.int32),
            pltpu.SMEM((CLIPS,), jnp.int32),
            pltpu.SMEM((CLIPS,), jnp.int32),
            pltpu.VMEM((CLIPS * TEXT, HEAD_DIM), BF16),
            pltpu.VMEM((CLIPS * TEXT, HEAD_DIM), BF16),
            pltpu.VMEM((ROWS, HEAD_DIM), BF16),
            pltpu.VMEM((ROWS + 2 * PAD, HEAD_DIM), BF16),
            pltpu.VMEM((CLIPS * TEXT, HEAD_DIM), BF16),
            pltpu.VMEM((CLIPS, ROWS), F32),
            pltpu.VMEM((CLIPS, ROWS), jnp.int32),
            pltpu.VMEM((CLIPS * CHANNELS, 2 * HEAD_DIM), BF16),
            pltpu.VMEM((CHANNELS, TOK), F32),
            pltpu.VMEM((CHANNELS, TOK), F32),
            pltpu.VMEM((CHANNELS, TOK), F32),
            pltpu.VMEM((ROWS, HEAD_DIM), F32),
            pltpu.VMEM((ROWS, HEAD_DIM), F32),
            pltpu.VMEM((ROWS, HEAD_DIM), F32),
            pltpu.VMEM((ROWS, HEAD_DIM), F32),
            pltpu.VMEM((12, 5 * BLOCK, BLOCK), BF16),
            pltpu.VMEM((12 * BLOCK, HEAD_DIM), F32),
            pltpu.VMEM((8, 2, MSG, TOK), BF16),
            pltpu.VMEM((8, MSG, TOK), BF16),
            pltpu.VMEM((8, MSG, TOK), BF16),
            pltpu.VMEM((N_SEQ, MSG, TOK), BF16),
            pltpu.VMEM((1, HEAD_DIM), F32),
            pltpu.VMEM((N_SEQ, 1, HEAD_DIM), F32),
            pltpu.VMEM((1, HEAD_DIM), F32),
            pltpu.VMEM((N_DP, 1, HEAD_DIM), F32),
            pltpu.SemaphoreType.REGULAR,
            pltpu.SemaphoreType.REGULAR,
            dma((9,)),
            dma((3,)),
            dma((2,)),
            dma((8,)),
            dma((1,)),
            dma((8,)),
            dma((1,)),
            dma((1,)),
            dma((1,)),
            dma((1,)),
            dma((1,)),
            dma((1,)),
        ],
        compiler_params=pltpu.CompilerParams(
            collective_id=0, has_side_effects=True, vmem_limit_bytes=40 * 1024 * 1024
        ),
    )(*[pltpu.with_memory_space_constraint(operand, pltpu.HBM) for operand in (
        queries, keys, values, text, text_lengths, clip_lengths, report_order, timesteps, mod_weight, final_weight.T, noise.T, clean.T
    )])
    return out[0, :CLIPS]


def solution(mesh):
    rows = P(("dp", "seq"), None)
    in_specs = (
        rows, rows, rows, P("dp", None, None, "seq"), P("dp"), P("dp", None), P("dp"), P(), P(), rows, rows, P("dp"),
    )
    return jax.shard_map(per_device, mesh=mesh, in_specs=in_specs, out_specs=P("dp"), check_vma=False)
```

```python
import functools
import math

import jax
import jax.numpy as jnp
from jax import lax
from jax.experimental import pallas as pl
from jax.experimental.pallas import tpu as pltpu
from jax.sharding import PartitionSpec as P

MESH = pl.DeviceIdType.MESH
HEAD_DIM = 128
FREQ = 256
CLIPS = 8
TEXT = 256
CHANNELS = 64
WIDTH = 2048
TOK = 128
N_SEQ = 16
N_DP = 32
ROWS = TOK * N_SEQ
BLOCK = 256
BLOCKS = ROWS // BLOCK
PAD = 512
WINDOW = BLOCK + 2 * PAD
NEAR_CLIPS = 5
SPAN = NEAR_CLIPS * TEXT
MSG = 80
FAR = 65536.0
EPS = 1e-06
SCALE = math.log2(math.e) / math.sqrt(HEAD_DIM)
NT = (((1,), (1,)), ((), ()))
F32 = jnp.float32
BF16 = jnp.bfloat16


def nt_dot(a, b):
    return lax.dot_general(a, b, NT, preferred_element_type=F32)


def nn_dot(a, b):
    return jnp.dot(a, b, preferred_element_type=F32)


def pieces(x, count):
    out = []
    for _ in range(count):
        piece = x.astype(BF16)
        out.append(piece)
        x = x - piece.astype(F32)
    return out


def along(scalars, shape, dim):
    place = lax.broadcasted_iota(jnp.int32, shape, dim)
    out = jnp.zeros(shape, jnp.int32)
    for index, scalar in enumerate(scalars):
        out = jnp.where(place == index, scalar, out)
    return out


PARTNERS = [(0, 1), (1, 0), (-1, 0), (1, 1), (-1, 1), (2, 0), (-2, 0), (2, 1), (-2, 1)]
NEAR = len(PARTNERS)
PARTNERS += [(3, 0), (-3, 0), (3, 1), (-3, 1), (4, 0), (4, 1)]


GROUPS = sorted(
    [(dx, dy) for dx in range(4) for dy in range(8) if dx or dy],
    key=lambda step: -(min(step[0], 4 - step[0]) + min(step[1], 8 - step[1])),
)
SOURCES = [0, 4, 3, -3, 2, -2, 1, -1]
EARLY = 6
FINISH = [4, -3, 3, 2, -2, 1, -1, 0]


def wait_for(buffer, sem):
    pltpu.make_async_copy(buffer, buffer, sem).wait()


def kernel(
    q_hbm, k_hbm, v_hbm, text_hbm, tlen_hbm, clen_hbm, order_hbm, time_hbm, modw_hbm, finw_hbm, noise_hbm, clean_hbm,
    out_ref,
    qbuf, kbuf, vbuf, textbuf, modw, finw, noise, clean, tlen_ref, clen_ref, order_ref, time_ref,
    tk, tv, qbias, kbias, tbias, onehot, clip_row, wall, btok, ctok, target,
    text_max, text_sum, text_out, inverse, weights, mixed_out, pair, taken, message, gathered, part_out, part_in, loss_out, loss_in,
    far_sem, cross_sem, load_sem, in_send, in_recv, value_recv, pair_send, pair_recv, msg_send, msg_recv, part_send, part_recv, loss_send, loss_recv,
):
    me = lax.axis_index("seq")
    dp = lax.axis_index("dp")
    z = me // 2
    core = me % 2
    peers = [lax.rem(z + dz + 8, 8) * 2 + lax.rem(core + dc, 2) for dz, dc in PARTNERS]

    barrier = pltpu.get_barrier_semaphore()
    for peer in peers[:NEAR]:
        pl.semaphore_signal(barrier, inc=1, device_id=(dp, peer), device_id_type=MESH)
    others = [lax.rem(dp // 8 + dx, 4) * 8 + lax.rem(lax.rem(dp, 8) + dy, 8) for dx, dy in GROUPS]
    across = [lax.rem(dp // 8 + i, 4) * 8 + lax.rem(dp, 8) for i in range(1, 4)]
    down = [dp // 8 * 8 + lax.rem(lax.rem(dp, 8) + i, 8) for i in range(1, 8)]
    for group in across + down:
        pl.semaphore_signal(barrier, inc=1, device_id=(group, me), device_id_type=MESH)

    streams = [(q_hbm, qbuf, 0), (k_hbm, kbuf, PAD), (v_hbm, vbuf, PAD)]
    pl.semaphore_wait(barrier, NEAR + len(across) + len(down))
    for dz in (2, -2):
        pl.semaphore_signal(far_sem, inc=1, device_id=(dp, lax.rem(z + dz + 8, 8) * 2 + core), device_id_type=MESH)
    for group in across:
        pl.semaphore_signal(cross_sem, inc=1, device_id=(group, me), device_id_type=MESH)

    def send_part(t, partners):
        src, dst, base = streams[t]
        for dz, dc in partners:
            peer = lax.rem(z + dz + 8, 8) * 2 + lax.rem(core + dc, 2)
            pltpu.make_async_remote_copy(
                src_ref=src.at[:, pl.ds(pl.multiple_of(peer * HEAD_DIM, HEAD_DIM), HEAD_DIM)],
                dst_ref=dst.at[pl.ds(pl.multiple_of(base + me * TOK, TOK), TOK)],
                send_sem=in_send.at[t],
                recv_sem=in_recv.at[t] if t < 2 else value_recv.at[dz % 8],
                device_id=(dp, peer),
                device_id_type=MESH,
            ).start()

    send_part(0, PARTNERS[:NEAR][::-1])
    pl.semaphore_wait(far_sem, 2)
    send_part(0, PARTNERS[NEAR:][::-1])
    loads = [
        pltpu.make_async_copy(src, dst, load_sem.at[i])
        for i, (src, dst) in enumerate(
            [
                (tlen_hbm, tlen_ref), (clen_hbm, clen_ref), (order_hbm, order_ref), (time_hbm, time_ref),
                (text_hbm, textbuf), (modw_hbm, modw), (finw_hbm, finw), (noise_hbm, noise), (clean_hbm, clean),
            ]
        )
    ]
    for load in loads:
        load.start()
    head_at = pl.multiple_of(me * HEAD_DIM, HEAD_DIM)
    for t, (src, dst, base) in enumerate(streams):
        pltpu.make_async_copy(
            src.at[:, pl.ds(head_at, HEAD_DIM)],
            dst.at[pl.ds(pl.multiple_of(base + me * TOK, TOK), TOK)],
            in_recv.at[t] if t < 2 else value_recv.at[0],
        ).start()

    send_part(1, PARTNERS[::-1])
    send_part(2, PARTNERS[::-1])
    for load in loads[:4]:
        load.wait()

    starts, ends = [], []
    total = jnp.int32(0)
    for c in range(CLIPS):
        starts.append(total)
        total = total + clen_ref[0, c]
        ends.append(total)
    start_lane, end_lane = along(starts, (1, HEAD_DIM), 1), along(ends, (1, HEAD_DIM), 1)
    start_col, end_col = along(starts, (CLIPS, 1), 0), along(ends, (CLIPS, 1), 0)
    size_row = jnp.where(end_lane > start_lane, end_lane - start_lane, 1).astype(F32)
    place = lax.broadcasted_iota(jnp.int32, (CLIPS, ROWS), 1)
    onehot[...] = jnp.where((place >= start_col) & (place < end_col), 1.0, 0.0)
    clip_of = jnp.zeros((CLIPS, ROWS), jnp.int32)
    for c in range(1, CLIPS):
        clip_of = clip_of + jnp.where(place >= starts[c], 1, 0)
    clip_row[...] = clip_of
    edge = jnp.zeros((PAD, HEAD_DIM), BF16)
    for buf in (kbuf, vbuf):
        buf[pl.ds(0, PAD), :] = edge
        buf[pl.ds(PAD + ROWS, PAD), :] = edge

    rows_iota = lax.broadcasted_iota(jnp.int32, (BLOCK, HEAD_DIM), 0)
    lane_iota = lax.broadcasted_iota(jnp.int32, (BLOCK, HEAD_DIM), 1)

    def fill_key_bias(i, _):
        token = rows_iota + (i * BLOCK - PAD)
        live = (token >= start_lane) & (token < end_lane)
        kbias[pl.ds(pl.multiple_of(i * BLOCK, BLOCK), BLOCK), :] = jnp.where(live, 0.0, -FAR).astype(BF16)
        return 0

    def fill_query_bias(i, _):
        token = rows_iota + i * BLOCK
        live = (token >= start_lane) & (token < end_lane)
        qbias[pl.ds(pl.multiple_of(i * BLOCK, BLOCK), BLOCK), :] = jnp.where(live, 1.0, 0.0).astype(BF16)
        return 0

    lax.fori_loop(0, (ROWS + 2 * PAD) // BLOCK, fill_key_bias, 0)
    lax.fori_loop(0, BLOCKS, fill_query_bias, 0)

    loads[4].wait()
    sub = lax.broadcasted_iota(jnp.int32, (TEXT, 2 * TEXT), 0)
    lane = lax.broadcasted_iota(jnp.int32, (TEXT, 2 * TEXT), 1)
    pick_key = jnp.where(lane == 2 * sub, 1.0, 0.0).astype(BF16)
    pick_value = jnp.where(lane == 2 * sub + 1, 1.0, 0.0).astype(BF16)
    length_lane = along([tlen_ref[c] for c in range(CLIPS)], (1, HEAD_DIM), 1)

    def split_text(c, _):
        both = textbuf[c]
        rows = pl.ds(pl.multiple_of(c * TEXT, TEXT), TEXT)
        tk[rows, :] = nn_dot(pick_key, both).astype(BF16)
        tv[rows, :] = nn_dot(pick_value, both).astype(BF16)
        live = (lane_iota == c) & (rows_iota < length_lane)
        tbias[rows, :] = jnp.where(live, 0.0, -FAR).astype(BF16)
        return 0

    lax.fori_loop(0, CLIPS, split_text, 0)

    loads[5].wait()
    loads[6].wait()
    step = along([time_ref[c] for c in range(CLIPS)], (CLIPS, FREQ // 2), 0).astype(F32)
    ramp = lax.broadcasted_iota(jnp.int32, (CLIPS, FREQ // 2), 1).astype(F32)
    angles = step * jnp.exp(-math.log(10000.0) * ramp / (FREQ // 2))
    embedding = jnp.concatenate([jnp.cos(angles), jnp.sin(angles)], axis=1)
    act = jax.nn.silu(embedding).astype(BF16)
    gain = 1.0 + nn_dot(act, modw[:, pl.ds(WIDTH + head_at, HEAD_DIM)])
    turned = finw[:, pl.ds(head_at, HEAD_DIM)].astype(F32)
    for c in range(CLIPS):
        high, low = pieces(turned * gain[c : c + 1, :], 2)
        wall[pl.ds(c * CHANNELS, CHANNELS), :] = jnp.concatenate([high, low], axis=1)
    shift_all = nn_dot(act, modw[:, pl.ds(0, WIDTH)])
    gain_all = 1.0 + nn_dot(act, modw[:, pl.ds(WIDTH, WIDTH)])
    stacked = jnp.concatenate(pieces(gain_all, 3) + pieces(shift_all, 3), axis=0)
    folded = nt_dot(finw[...], stacked)
    gain_sum = folded[:, 0:8] + folded[:, 8:16] + folded[:, 16:24]
    shift_sum = folded[:, 24:32] + folded[:, 32:40] + folded[:, 40:48]
    mine = onehot[:, pl.ds(pl.multiple_of(me * TOK, TOK), TOK)]
    gain_tok = jnp.zeros((CHANNELS, TOK), F32)
    shift_tok = jnp.zeros((CHANNELS, TOK), F32)
    for c in range(CLIPS):
        gain_tok = gain_tok + gain_sum[:, c : c + 1] * mine[c : c + 1, :]
        shift_tok = shift_tok + shift_sum[:, c : c + 1] * mine[c : c + 1, :]
    btok[...] = gain_tok
    ctok[...] = shift_tok
    loads[7].wait()
    loads[8].wait()
    target[...] = noise[...] - clean[...]
    order_col = along([order_ref[c] for c in range(CLIPS)], (CLIPS, HEAD_DIM), 0)
    order_lane = lax.broadcasted_iota(jnp.int32, (CLIPS, HEAD_DIM), 1)
    wanted = jnp.where(order_lane < CLIPS, order_col - order_lane, -1)

    wait_for(qbuf, in_recv.at[0])
    one_lanes = jnp.ones((SPAN, HEAD_DIM), BF16)

    def text_block(b, _):
        rows = pl.ds(pl.multiple_of(b * BLOCK, BLOCK), BLOCK)
        span = pl.ds(pl.multiple_of(b // 2 * TEXT, TEXT), SPAN)
        left = jnp.concatenate([qbuf[rows, :], qbias[rows, :]], axis=1)
        right = jnp.concatenate([tk[span, :], tbias[span, :]], axis=1)
        scores = nt_dot(left, right)
        top = jnp.max(scores, axis=1, keepdims=True)
        weight = jnp.exp2((scores - top) * SCALE).astype(BF16)
        mixed = nn_dot(weight, jnp.concatenate([tv[span, :], one_lanes], axis=1))
        text_max[rows, :] = jnp.broadcast_to(top, (BLOCK, HEAD_DIM))
        text_out[rows, :] = mixed[:, :HEAD_DIM]
        text_sum[rows, :] = mixed[:, HEAD_DIM:]
        return 0

    lax.fori_loop(0, BLOCKS, text_block, 0)

    wait_for(kbuf.at[pl.ds(PAD, ROWS)], in_recv.at[1])

    def score_block(b, _):
        rows = pl.ds(pl.multiple_of(b * BLOCK, BLOCK), BLOCK)
        window = pl.ds(pl.multiple_of(b * BLOCK, BLOCK), WINDOW)
        left = jnp.concatenate([qbuf[rows, :], qbias[rows, :]], axis=1)
        right = jnp.concatenate([kbuf[window, :], kbias[window, :]], axis=1)
        scores = nt_dot(left, right)
        before = text_max[rows, :]
        top = jnp.maximum(before, jnp.max(scores, axis=1, keepdims=True))
        weight = jnp.exp2((scores - top[:, :1]) * SCALE)
        video_sum = jnp.sum(weight, axis=1, keepdims=True)
        weight = weight.astype(BF16)
        for t in range(5):
            weights[b + t, pl.ds((4 - t) * BLOCK, BLOCK), :] = weight[:, t * BLOCK : (t + 1) * BLOCK]
        fade = jnp.exp2((before - top) * SCALE)
        inv = 1.0 / (video_sum + text_sum[rows, :] * fade)
        inverse[rows, :] = inv
        text_out[rows, :] = text_out[rows, :] * (fade * inv)
        return 0

    lax.fori_loop(0, BLOCKS, score_block, 0, unroll=2)

    mixed_out[...] = jnp.zeros(mixed_out.shape, F32)

    def value_rows(dz):
        chip = lax.rem(z - dz + 8, 8)
        wait_for(vbuf.at[pl.ds(PAD, BLOCK)], value_recv.at[dz % 8])
        return chip, vbuf[pl.ds(pl.multiple_of(PAD + chip * BLOCK, BLOCK), BLOCK), :]

    def add_source(dz):
        chip, rows = value_rows(dz)
        around = pl.ds(pl.multiple_of(chip * BLOCK, BLOCK), 5 * BLOCK)
        mixed_out[around, :] = mixed_out[around, :] + nn_dot(weights[chip + 2], rows)

    ones_rows = jnp.ones((16, HEAD_DIM), BF16)
    zero_rows = jnp.zeros((16, HEAD_DIM), BF16)
    count_left = jnp.concatenate([ones_rows, zero_rows], axis=1)
    count_both = jnp.concatenate([ones_rows, ones_rows], axis=1)
    row16 = lax.broadcasted_iota(jnp.int32, (16, TOK), 0)
    wide16 = lax.broadcasted_iota(jnp.int32, (16, BLOCK), 0)

    def stat_rows(place, total, squares):
        rows = jnp.zeros(place.shape, F32)
        for at, piece in enumerate(pieces(total, 3) + pieces(squares, 3)):
            rows = jnp.where(place == at, piece.astype(F32), rows)
        return rows

    def read_stats(rows):
        return rows[64:65] + rows[65:66] + rows[66:67], rows[67:68] + rows[68:69] + rows[69:70]

    def project(b):
        rows = pl.ds(pl.multiple_of(b * BLOCK, BLOCK), BLOCK)
        first = b // 2
        mixed = mixed_out[pl.ds(pl.multiple_of((b + 2) * BLOCK, BLOCK), BLOCK), :]
        attended = (mixed * inverse[rows, :] + text_out[rows, :]).astype(BF16)
        fold = wall[pl.ds(pl.multiple_of(first * CHANNELS, CHANNELS), NEAR_CLIPS * CHANNELS), :]
        spread = nt_dot(jnp.concatenate([fold, count_left], axis=0), jnp.concatenate([attended, attended], axis=1))
        clip_here = clip_row[0:1, rows]
        picked = spread[:CHANNELS]
        for j in range(1, NEAR_CLIPS):
            picked = jnp.where(clip_here == first + j, spread[j * CHANNELS : (j + 1) * CHANNELS], picked)
        wide = attended.astype(F32)
        squares = nt_dot(count_both, jnp.concatenate(pieces(wide * wide, 2), axis=1))
        stats = stat_rows(wide16, spread[NEAR_CLIPS * CHANNELS :], squares)
        full = jnp.concatenate([picked, stats], axis=0).astype(BF16)
        pair[b, 0] = full[:, :TOK]
        pair[b, 1] = full[:, TOK:]

    def exchange(i, b):
        copy = pltpu.make_async_remote_copy(
            src_ref=pair.at[b, 1 - core],
            dst_ref=taken.at[b],
            send_sem=pair_send.at[0],
            recv_sem=pair_recv.at[i],
            device_id=(dp, z * 2 + 1 - core),
            device_id_type=MESH,
        )
        copy.start()
        return copy

    def message_copy(source, slot, owner):
        pltpu.make_async_remote_copy(
            src_ref=source,
            dst_ref=gathered.at[slot],
            send_sem=msg_send.at[0],
            recv_sem=msg_recv.at[0],
            device_id=(dp, owner),
            device_id_type=MESH,
        ).start()

    def deliver(i, b, copy):
        copy.wait_recv()
        both = pair[b, core].astype(F32) + taken[b].astype(F32)
        stats = stat_rows(row16, *read_stats(both))
        total = jnp.concatenate([both[:CHANNELS], stats], axis=0).astype(BF16)
        if FINISH[i] == 0:
            gathered[2 * z] = total
            return
        message[b] = total
        message_copy(message.at[b], 2 * z, b * 2 + core)

    def finish(i):
        b = lax.rem(z + FINISH[i] + 8, 8)
        project(b)
        return i, b, exchange(i, b)

    for dz in SOURCES[:EARLY]:
        add_source(dz)
    waiting = [finish(0)]
    add_source(SOURCES[EARLY])
    waiting.append(finish(1))
    deliver(*waiting[0])
    add_source(SOURCES[EARLY + 1])
    for i in range(2, len(FINISH)):
        waiting.append(finish(i))
    for entry in waiting[1:]:
        deliver(*entry)

    wait_for(gathered.at[pl.ds(0, 7)], msg_recv.at[0])
    total = gathered[2 * z].astype(F32)
    for dz in (1, 2, 3, 4, 5, 6, 7):
        chip = lax.rem(z + dz, 8)
        total = total + gathered[2 * chip].astype(F32)
    features, squares = read_stats(total)
    center = features / WIDTH
    spread = squares / WIDTH - center * center
    predicted = lax.rsqrt(spread + EPS) * (total[:CHANNELS] - center * btok[...]) + ctok[...]
    difference = predicted - target[...]
    error = jnp.sum(difference * difference, axis=0, keepdims=True) / CHANNELS
    mine = onehot[:, pl.ds(pl.multiple_of(me * TOK, TOK), TOK)]
    slot = lax.broadcasted_iota(jnp.int32, (CLIPS, HEAD_DIM), 0)
    lanes = lax.broadcasted_iota(jnp.int32, (CLIPS, HEAD_DIM), 1)
    partial = jnp.sum(mine * error, axis=1, keepdims=True)
    partial = jnp.sum(jnp.where(slot == lanes, partial, 0.0), axis=0, keepdims=True)
    part_out[...] = partial
    for peer in reversed(peers):
        pltpu.make_async_remote_copy(
            src_ref=part_out,
            dst_ref=part_in.at[me],
            send_sem=part_send.at[0],
            recv_sem=part_recv.at[0],
            device_id=(dp, peer),
            device_id_type=MESH,
        ).start()
    part_in[me] = partial
    wait_for(part_in.at[pl.ds(0, N_SEQ - 1)], part_recv.at[0])
    partial = part_in[0]
    for rank in range(1, N_SEQ):
        partial = partial + part_in[rank]
    losses = partial / size_row
    pl.semaphore_wait(cross_sem, len(across))
    loss_out[...] = losses
    for group in others:
        pltpu.make_async_remote_copy(
            src_ref=loss_out,
            dst_ref=loss_in.at[dp],
            send_sem=loss_send.at[0],
            recv_sem=loss_recv.at[0],
            device_id=(group, me),
            device_id_type=MESH,
        ).start()
    loss_in[dp] = losses
    wait_for(loss_in.at[pl.ds(0, N_DP - 1)], loss_recv.at[0])
    scores = jnp.zeros((CLIPS, HEAD_DIM), F32)
    for group in range(N_DP):
        scores = scores + jnp.where(wanted == group * CLIPS, loss_in[group], 0.0)
    scores = jnp.sum(scores, axis=1, keepdims=True)
    out_ref[...] = jnp.sum(jnp.where(slot == lanes, scores, 0.0), axis=0, keepdims=True)

    for t in range(3):
        wait_for(qbuf.at[pl.ds(0, (N_SEQ - 1) * TOK)], in_send.at[t])
    wait_for(taken.at[pl.ds(0, 8)], pair_send.at[0])
    wait_for(gathered.at[pl.ds(0, 7)], msg_send.at[0])
    wait_for(part_in.at[pl.ds(0, N_SEQ - 1)], part_send.at[0])
    wait_for(loss_in.at[pl.ds(0, N_DP - 1)], loss_send.at[0])


def per_device(
    queries, keys, values, text_kv, text_lengths, clip_lengths, timesteps, mod_weight, final_weight, noise, clean, report_order
):
    text = text_kv.reshape(CLIPS, 2 * TEXT, HEAD_DIM)
    anywhere = pl.BlockSpec(memory_space=pl.ANY)
    vmem = pl.BlockSpec(memory_space=pltpu.VMEM)
    dma = pltpu.SemaphoreType.DMA
    out = pl.pallas_call(
        kernel,
        out_shape=jax.ShapeDtypeStruct((1, HEAD_DIM), F32),
        in_specs=[anywhere] * 12,
        out_specs=vmem,
        scratch_shapes=[
            pltpu.VMEM((ROWS, HEAD_DIM), BF16),
            pltpu.VMEM((ROWS + 2 * PAD, HEAD_DIM), BF16),
            pltpu.VMEM((ROWS + 2 * PAD, HEAD_DIM), BF16),
            pltpu.VMEM((CLIPS, 2 * TEXT, HEAD_DIM), BF16),
            pltpu.VMEM((FREQ, 2 * WIDTH), BF16),
            pltpu.VMEM((CHANNELS, WIDTH), BF16),
            pltpu.VMEM((CHANNELS, TOK), F32),
            pltpu.VMEM((CHANNELS, TOK), F32),
            pltpu.SMEM((CLIPS,), jnp.int32),
            pltpu.SMEM((1, CLIPS), jnp.int32),
            pltpu.SMEM((CLIPS,), jnp.int32),
            pltpu.SMEM((CLIPS,), jnp.int32),
            pltpu.VMEM((CLIPS * TEXT, HEAD_DIM), BF16),
            pltpu.VMEM((CLIPS * TEXT, HEAD_DIM), BF16),
            pltpu.VMEM((ROWS, HEAD_DIM), BF16),
            pltpu.VMEM((ROWS + 2 * PAD, HEAD_DIM), BF16),
            pltpu.VMEM((CLIPS * TEXT, HEAD_DIM), BF16),
            pltpu.VMEM((CLIPS, ROWS), F32),
            pltpu.VMEM((CLIPS, ROWS), jnp.int32),
            pltpu.VMEM((CLIPS * CHANNELS, 2 * HEAD_DIM), BF16),
            pltpu.VMEM((CHANNELS, TOK), F32),
            pltpu.VMEM((CHANNELS, TOK), F32),
            pltpu.VMEM((CHANNELS, TOK), F32),
            pltpu.VMEM((ROWS, HEAD_DIM), F32),
            pltpu.VMEM((ROWS, HEAD_DIM), F32),
            pltpu.VMEM((ROWS, HEAD_DIM), F32),
            pltpu.VMEM((ROWS, HEAD_DIM), F32),
            pltpu.VMEM((12, 5 * BLOCK, BLOCK), BF16),
            pltpu.VMEM((12 * BLOCK, HEAD_DIM), F32),
            pltpu.VMEM((8, 2, MSG, TOK), BF16),
            pltpu.VMEM((8, MSG, TOK), BF16),
            pltpu.VMEM((8, MSG, TOK), BF16),
            pltpu.VMEM((N_SEQ, MSG, TOK), BF16),
            pltpu.VMEM((1, HEAD_DIM), F32),
            pltpu.VMEM((N_SEQ, 1, HEAD_DIM), F32),
            pltpu.VMEM((1, HEAD_DIM), F32),
            pltpu.VMEM((N_DP, 1, HEAD_DIM), F32),
            pltpu.SemaphoreType.REGULAR,
            pltpu.SemaphoreType.REGULAR,
            dma((9,)),
            dma((3,)),
            dma((2,)),
            dma((8,)),
            dma((1,)),
            dma((8,)),
            dma((1,)),
            dma((1,)),
            dma((1,)),
            dma((1,)),
            dma((1,)),
            dma((1,)),
        ],
        compiler_params=pltpu.CompilerParams(
            collective_id=0, has_side_effects=True, vmem_limit_bytes=40 * 1024 * 1024
        ),
    )(*[pltpu.with_memory_space_constraint(operand, pltpu.HBM) for operand in (
        queries, keys, values, text, text_lengths, clip_lengths, report_order, timesteps, mod_weight, final_weight.T, noise.T, clean.T
    )])
    return out[0, :CLIPS]


def solution(mesh):
    rows = P(("dp", "seq"), None)
    in_specs = (
        rows, rows, rows, P("dp", None, None, "seq"), P("dp"), P("dp", None), P("dp"), P(), P(), rows, rows, P("dp"),
    )
    return jax.shard_map(per_device, mesh=mesh, in_specs=in_specs, out_specs=P("dp"), check_vma=False)
```
